128 devices in a mesh: row: 16 (over x, z), col: 8 (over y, core).
Axes of the slice: x: 4, y: 4, z: 4, core: 2. Of those that a mesh axis runs over, the one named last changes fastest.
Arguments:
- charge_drive: float32 [512, 16, 128], P(('row', 'col')), may hold values from -6 to 6
- hardness: float32 [512, 128], P(('row', 'col')), may hold values from 1 to 4
- bond_stiffness: float32 [1024, 128], P('row'), may hold values from 0.5 to 4
- coulomb_tiles: float32 [16384, 128, 128], P(('row', 'col')), may hold values from -0.01 to 0.01
- tile_rows: int32 [16384], P(('row', 'col')), may hold values from 0 to 63
- tile_cols: int32 [16384], P(('row', 'col')), may hold values from 0 to 31
- tile_count: int32 [128], P(('row', 'col')), may hold values from 25 to 128, as said below
- link_bonds: int32 [4096], P(('row', 'col')), may hold values from 0 to 63, as said below
- link_cells: int32 [4096], P(('row', 'col')), may hold values from 0 to 63
- link_ends: int32 [4096, 2, 128], P(('row', 'col')), may hold values from 0 to 127, as said below
- link_carry: int32 [4096, 128], P(('row', 'col')), may hold values from 0 to 1, as said below
- link_count: int32 [128], P(('row', 'col')), may hold values from 8 to 32, as said below
Outputs:
- solution: float32 [1024, 16, 128], P(('row', 'col'))
- residual: float32 [1024, 16, 128], P(('row', 'col'))
The draws below stay inside these ranges and needn't reach their ends.
Inputs may be any that keep to these rules, and one draw needn't show every extreme that they name: `tile_count`: live tile slots of each device, the busiest device has exactly 128. `link_count`: live incidence slots of each device, the busiest device has exactly 32. `link_bonds`: within each row of devices, every bond of every one of the row's bond blocks is carried by exactly one live incidence slot. `link_carry`: dead slots carry nothing. `link_ends`: the two ends of every bond are distinct atoms.
All inputs are finite; a program needn't handle non-finite values.
Results may differ from the reference program's by a relative error of at most 0.00022.
Values sent between devices are 32-bit elements; how exact they have to be, the bound alone decides.
No kernel may reach another device: no remote copies, remote signals or barrier semaphores. Data moves between devices by JAX's collectives and lax.ppermute only.
A program may use at most 64 MiB of HBM per device.

```python
import math
import jax
import jax.numpy as jnp
from jax import lax

CELLS_DEV = 4
SETS = 16
CELL_ATOMS = 128
ITERS = 2
GRID_COLS = 8
OWNERS = 128
TILE_SLOTS = 128
LINK_SLOTS = 32
R_CELLS = 64
C_CELLS = 32
ROW_BONDS = 64
NCELLS = 512
NBONDS = 1024


def skewed_counts(key, slots, widest):
    first_key, second_key = jax.random.split(key)
    divisor = jax.random.randint(first_key, (OWNERS,), 1, widest + 1)
    counts = slots // divisor
    busiest = jax.random.randint(second_key, (), 0, OWNERS)
    return counts.at[busiest].set(slots).astype(jnp.int32)


def link_layout(key):
    counts = skewed_counts(jax.random.fold_in(key, 23), LINK_SLOTS, 4)
    group_rows = OWNERS // GRID_COLS
    slot_grid = counts.reshape(group_rows, GRID_COLS)
    before = jnp.cumsum(slot_grid, axis=1) - slot_grid
    slot_ids = jnp.arange(LINK_SLOTS, dtype=jnp.int32)
    row_order = (before[:, :, None] + slot_ids[None, None, :]).reshape(group_rows, GRID_COLS * LINK_SLOTS)
    alive_slots = (slot_ids[None, None, :] < slot_grid[:, :, None]).reshape(group_rows, GRID_COLS * LINK_SLOTS)
    live_total = jnp.sum(slot_grid, axis=1)
    position = row_order % ROW_BONDS
    rank_in_block = row_order // ROW_BONDS
    row_keys = jax.random.split(jax.random.fold_in(key, 29), group_rows)
    shuffles = jax.vmap(lambda sub_key: jax.random.permutation(sub_key, ROW_BONDS))(row_keys)
    blocks = jax.vmap(lambda table, where: table[where])(shuffles, position)
    block_ids = jnp.arange(ROW_BONDS, dtype=jnp.int32)
    holders = (live_total[:, None] - block_ids[None, :] - 1) // ROW_BONDS + 1
    holder_picks = jax.random.randint(jax.random.fold_in(key, 31), (group_rows, ROW_BONDS, CELL_ATOMS), 0, holders[:, :, None])
    chosen = jax.vmap(lambda table, where: table[where])(holder_picks, position)
    carried = (chosen == rank_in_block[:, :, None]) & alive_slots[:, :, None]
    carried = carried.astype(jnp.int32).reshape(OWNERS * LINK_SLOTS, CELL_ATOMS)
    return (counts, blocks.reshape(OWNERS * LINK_SLOTS).astype(jnp.int32), carried)


def draw_tile_count(key, part):
    return skewed_counts(jax.random.fold_in(key, 11), TILE_SLOTS, 5)


def draw_link_count(key, part):
    return link_layout(key)[0]


def draw_link_bonds(key, part):
    return link_layout(key)[1]


def draw_link_carry(key, part):
    return link_layout(key)[2]


def draw_link_ends(key, part):
    first_key, second_key = jax.random.split(jax.random.fold_in(key, 37))
    gainer = jax.random.randint(first_key, (OWNERS * LINK_SLOTS, CELL_ATOMS), 0, CELL_ATOMS)
    offset = jax.random.randint(second_key, (OWNERS * LINK_SLOTS, CELL_ATOMS), 1, CELL_ATOMS)
    loser = (gainer + offset) % CELL_ATOMS
    return jnp.stack([gainer, loser], axis=1).astype(jnp.int32)


def place_ends(drawn, stream_key, least, top_value):
    longest = drawn.shape.index(max(drawn.shape))
    spots = []
    for shift in (0, 1):
        where = [jax.random.randint(jax.random.fold_in(stream_key, axis), (), 0, length) for axis, length in enumerate(drawn.shape)]
        where[longest] = (where[longest] + shift) % drawn.shape[longest]
        spots.append(tuple(where))
    return drawn.at[spots[0]].set(least).at[spots[1]].set(top_value)


def steps_of(key, extent, cuts, smallest, top_value):
    gain, own = 1.0, jax.random.fold_in(key, 6)
    for axis_at, shards_of in cuts:
        draws = jnp.exp(jax.random.uniform(jax.random.fold_in(own, axis_at), (shards_of,), jnp.float32, smallest / len(cuts), top_value / len(cuts)))
        gain = gain * jnp.repeat(draws, extent[axis_at] // shards_of).reshape([-1 if axis == axis_at else 1 for axis in range(len(extent))])
    return gain


def bell_draw(rng, dims, deviation, reach, pieces=(), kind=jnp.bfloat16):
    level = steps_of(rng, dims, pieces, -0.22, 0.18) if pieces else 1.0
    values = jax.random.normal(rng, dims, jnp.float32) * deviation * level
    return jnp.minimum(jnp.maximum(values, -reach), reach).astype(kind)


def setup_inputs(seed: int = 0) -> dict:
    key_list = jax.random.split(jax.random.key(seed), 13)
    charge_drive = bell_draw(key_list[0], (NCELLS, SETS, CELL_ATOMS), 1.0, 6.0, ((0, 128),), jnp.float32)
    hardness = jnp.clip(jnp.exp(math.log(4.0) - 1.3862944 * jax.random.uniform(key_list[1], (NCELLS, CELL_ATOMS), jnp.float32) ** steps_of(key_list[1], (NCELLS, CELL_ATOMS), ((0, 128),), -0.2, 0.2)), 1.0, 4.0)
    bond_stiffness = jnp.clip(jnp.exp(math.log(4.0) - 2.0794415 * jax.random.uniform(key_list[2], (NBONDS, CELL_ATOMS), jnp.float32) ** steps_of(key_list[2], (NBONDS, CELL_ATOMS), ((0, 16),), -0.2, 0.2)), 0.5, 4.0)
    coulomb_tiles = jnp.clip(jax.random.uniform(key_list[3], (OWNERS * TILE_SLOTS, CELL_ATOMS, CELL_ATOMS), jnp.float32, -0.01, 0.01) * steps_of(key_list[3], (OWNERS * TILE_SLOTS, CELL_ATOMS, CELL_ATOMS), ((0, 128),), -0.4, 0.0), -0.01, 0.01)
    tile_rows = place_ends(jax.random.randint(key_list[4], (OWNERS * TILE_SLOTS,), 0, R_CELLS), jax.random.fold_in(key_list[4], 1), 0, R_CELLS - 1).astype(jnp.int32)
    tile_cols = place_ends(jax.random.randint(key_list[5], (OWNERS * TILE_SLOTS,), 0, C_CELLS), jax.random.fold_in(key_list[5], 1), 0, C_CELLS - 1).astype(jnp.int32)
    tile_count = draw_tile_count(jax.random.fold_in(key_list[12], 71), 0)
    link_bonds = draw_link_bonds(jax.random.fold_in(key_list[12], 71), 0)
    link_cells = place_ends(jax.random.randint(key_list[8], (OWNERS * LINK_SLOTS,), 0, R_CELLS), jax.random.fold_in(key_list[8], 1), 0, R_CELLS - 1).astype(jnp.int32)
    link_ends = draw_link_ends(jax.random.fold_in(key_list[12], 71), 0)
    link_carry = draw_link_carry(jax.random.fold_in(key_list[12], 71), 0)
    link_count = draw_link_count(jax.random.fold_in(key_list[12], 71), 0)
    return {"charge_drive": charge_drive, "hardness": hardness, "bond_stiffness": bond_stiffness, "coulomb_tiles": coulomb_tiles, "tile_rows": tile_rows, "tile_cols": tile_cols, "tile_count": tile_count, "link_bonds": link_bonds, "link_cells": link_cells, "link_ends": link_ends, "link_carry": link_carry, "link_count": link_count}


highest = lax.Precision.HIGHEST


def reference(charge_drive, hardness, bond_stiffness, coulomb_tiles, tile_rows, tile_cols, tile_count, link_bonds, link_cells, link_ends, link_carry, link_count):
    total_cells = hardness.shape[0]
    total_bonds = bond_stiffness.shape[0]
    tile_slot = jnp.arange(coulomb_tiles.shape[0], dtype=jnp.int32)
    tile_owner = tile_slot // TILE_SLOTS
    tile_live = ((tile_slot % TILE_SLOTS) < tile_count[tile_owner]).astype(jnp.float32)
    tile_grid_row = tile_owner // GRID_COLS
    tile_grid_col = tile_owner % GRID_COLS
    target_cell = ((tile_rows // CELLS_DEV) * GRID_COLS + tile_grid_col) * CELLS_DEV + tile_rows % CELLS_DEV
    source_cell = (tile_grid_row * GRID_COLS + tile_cols // CELLS_DEV) * CELLS_DEV + tile_cols % CELLS_DEV
    link_slot = jnp.arange(link_bonds.shape[0], dtype=jnp.int32)
    link_owner = link_slot // LINK_SLOTS
    link_live = ((link_slot % LINK_SLOTS) < link_count[link_owner]).astype(jnp.float32)
    link_grid_row = link_owner // GRID_COLS
    link_grid_col = link_owner % GRID_COLS
    link_cell_global = ((link_cells // CELLS_DEV) * GRID_COLS + link_grid_col) * CELLS_DEV + link_cells % CELLS_DEV
    link_bond_global = link_grid_row * ROW_BONDS + link_bonds
    atom_ids = jnp.arange(128, dtype=jnp.int32)
    incidence = ((link_ends[:, 0, :, None] == atom_ids).astype(jnp.float32)
                 - (link_ends[:, 1, :, None] == atom_ids).astype(jnp.float32))
    incidence = incidence * link_live[:, None, None] * link_carry.astype(jnp.float32)[:, :, None]

    def bond_to_charge(bonds):
        parts = jnp.einsum("sba,sxb->sxa", incidence, bonds[link_bond_global], precision=highest)
        return jax.ops.segment_sum(parts, link_cell_global, num_segments=total_cells)

    def charge_to_bond(potential):
        parts = jnp.einsum("sba,sxa->sxb", incidence, potential[link_cell_global], precision=highest)
        return jax.ops.segment_sum(parts, link_bond_global, num_segments=total_bonds)

    def coulomb(charge):
        products = jnp.einsum("tij,txj->txi", coulomb_tiles, charge[source_cell], precision=highest)
        products = products * tile_live[:, None, None]
        mirrored = jnp.einsum("tij,txi->txj", coulomb_tiles, charge[target_cell], precision=highest)
        mirrored = mirrored * tile_live[:, None, None]
        return (hardness[:, None, :] * charge
                + jax.ops.segment_sum(products, target_cell, num_segments=total_cells)
                + jax.ops.segment_sum(mirrored, source_cell, num_segments=total_cells))

    def operate(direction):
        return charge_to_bond(coulomb(bond_to_charge(direction))) + bond_stiffness[:, None, :] * direction

    def totals(values):
        return jnp.sum(values, axis=(0, 2))

    right_side = -charge_to_bond(charge_drive)
    solution = jnp.zeros_like(right_side)
    residual = right_side
    direction = right_side
    norm_now = totals(residual * residual)
    for iteration in range(ITERS):
        applied = operate(direction)
        step_size = (norm_now / totals(direction * applied))[None, :, None]
        solution = solution + step_size * direction
        residual = residual - step_size * applied
        norm_next = totals(residual * residual)
        direction = residual + (norm_next / norm_now)[None, :, None] * direction
        norm_now = norm_next
    return solution, residual
```

```python
import jax
import jax.numpy as jnp
from jax import lax
from jax.experimental import pallas as pl
from jax.experimental.pallas import tpu as pltpu
from jax.sharding import Mesh, PartitionSpec as P

f32 = jnp.float32
bf16 = jnp.bfloat16
ROW = ("x", "z")
ALL = ("x", "z", "y", "core")
NN = (((1,), (0,)), ((), ()))
NT = (((1,), (1,)), ((), ()))
SMEM = pl.BlockSpec(memory_space=pltpu.SMEM)
VMEM = pl.BlockSpec(memory_space=pltpu.VMEM)
ANY = pl.BlockSpec(memory_space=pl.ANY)
META = 96
PAY = 104


def shape(*dims):
    return jax.ShapeDtypeStruct(dims, f32)


def params(mib):
    return pltpu.CompilerParams(vmem_limit_bytes=mib << 20)


def split(values):
    high = values.astype(bf16)
    return high, (values - high.astype(f32)).astype(bf16)


def stacked(values):
    high, low = split(values)
    return jnp.concatenate([high, low], 0)


def dot(a, b, dims):
    return lax.dot_general(a, b, dims, preferred_element_type=f32)


def ends_matrix(gain, lose):
    atoms = lax.broadcasted_iota(jnp.int32, (128, 128), 0).astype(f32)
    one, zero = f32(1.0), f32(0.0)
    return (jnp.where(atoms == gain, one, zero) - jnp.where(atoms == lose, one, zero)).astype(bf16)


def pack_kernel(bonds, count, cells, ends, carry, stiff, out, own, cell_row):
    live = count[0]
    slot = lax.broadcasted_iota(jnp.int32, (32, 128), 0)
    carried = (carry[...] > 0) & (slot < live)
    own[0:32] = jnp.where(carried, ends[:, 0, :].astype(f32), -1.0)
    own[32:64] = jnp.where(carried, ends[:, 1, :].astype(f32), -1.0)
    for s in range(32):
        own[64 + s : 65 + s] = stiff[pl.ds(bonds[s], 1), :]
    own[64:96] = jnp.where(carried, own[64:96], 0.0)
    cell_row[...] = jnp.zeros_like(cell_row)
    cell_row[0:1, 0:32] = cells[...]
    lane = lax.broadcasted_iota(jnp.int32, (8, 128), 1)
    own[META:PAY] = jnp.where(lane == 32, live, jnp.where(lane < live, cell_row[...], -1)).astype(f32)
    for k in range(16):
        out[k] = own[...]


def pack(bonds, count, cells, ends, carry, stiff):
    return pl.pallas_call(
        pack_kernel,
        out_shape=(shape(16, PAY, 128), shape(PAY, 128)),
        in_specs=[SMEM, SMEM, VMEM, VMEM, VMEM, VMEM],
        out_specs=(VMEM, VMEM),
        scratch_shapes=[pltpu.VMEM((8, 128), jnp.int32)],
        compiler_params=params(8),
        name="pack_links",
    )(bonds, count, cells, ends, carry, stiff)


def slot_rows(pay, item):
    k, s = item // 32, item % 32
    return pay[k, pl.ds(s, 1), :], pay[k, pl.ds(32 + s, 1), :], pay[k, pl.ds(64 + s, 1), :]


GROUP = 4


def first_kernel(pos, meta, pay, drive, items, places, number, q_copies, q_own, left, total):
    base = pos[0] * 4

    def scan_sender(k, n):
        def scan_slot(s, n):
            place = meta[k * 33 + s] - base
            items[n] = k * 32 + s
            places[n] = place
            return n + jnp.where((place >= 0) & (place < 4), 1, 0)

        return lax.fori_loop(0, meta[k * 33 + 32], scan_slot, n)

    n = lax.fori_loop(0, 16, scan_sender, 0)
    number[0] = n
    for i in range(4):
        left[i] = stacked(drive[i])
    total[...] = jnp.zeros_like(total)

    def group(g, carry):
        done = []
        for u in range(GROUP):
            t = g * GROUP + u
            valid = t < n
            item = jnp.where(valid, items[t], 0)
            place = jnp.where(valid, places[t], 4)
            gain, lose, _ = slot_rows(pay, item)
            matrix = ends_matrix(gain, lose)
            u2 = dot(left[jnp.minimum(place, 3)], matrix, NN)
            back = dot(stacked(-(u2[:16] + u2[16:])), matrix, NT)
            done.append((place, back[:16] + back[16:]))
        for place, back in done:
            total[place] = total[place] + back
        return carry

    lax.fori_loop(0, (n + GROUP - 1) // GROUP, group, 0)
    q_own[...] = total[0:4]
    for k in range(16):
        q_copies[k] = total[0:4]


def first(pos, meta, pay, drive):
    return pl.pallas_call(
        first_kernel,
        out_shape=(
            jax.ShapeDtypeStruct((520,), jnp.int32),
            jax.ShapeDtypeStruct((520,), jnp.int32),
            jax.ShapeDtypeStruct((1,), jnp.int32),
            shape(16, 4, 16, 128),
            shape(4, 16, 128),
        ),
        in_specs=[SMEM, SMEM, VMEM, VMEM],
        out_specs=(SMEM, SMEM, SMEM, VMEM, VMEM),
        scratch_shapes=[pltpu.VMEM((4, 32, 128), bf16), pltpu.VMEM((5, 16, 128), f32)],
        compiler_params=params(16),
        name="first_charges",
    )(pos, meta, pay, drive)


CHUNK = 8
TILES = 128


def tiles_kernel(pos, count, rows, cols, target, own, near, y1, y2, y3, sums, tiles,
                 pot_out, keep, send, buf, sems, left_s, left_t, pot, mir):
    def fetch(k):
        part = pl.ds(k * CHUNK, CHUNK)
        return pltpu.make_async_copy(tiles.at[part], buf.at[part], sems.at[k])

    for k in range(TILES // CHUNK):
        fetch(k).start()
    y, core = pos[1], pos[2]

    def put(ref, at, values):
        high, low = split(values)
        ref[at, 0:16, 0:128] = high
        ref[at, 16:32, 0:128] = low
        ref[at, 0:16, 128:256] = high
        ref[at, 16:32, 128:256] = jnp.zeros_like(low)

    for i in range(64):
        put(left_t, i, target[i])
    mine = (y * 2 + core) * 4
    other = (y * 2 + 1 - core) * 4
    for i in range(4):
        put(left_s, mine + i, own[i])
        put(left_s, other + i, near[i])
    for k, piece in ((1, y1), (2, y2), (3, y3)):
        there = (y + 4 - k) % 4
        for i in range(4):
            put(left_s, (there * 2 + core) * 4 + i, piece[i])
            put(left_s, (there * 2 + 1 - core) * 4 + i, piece[4 + i])
    pot[...] = jnp.zeros_like(pot)
    mir[...] = jnp.zeros_like(mir)
    live = count[0]

    def group(g, carry):
        fetch(g).wait()
        done = []
        for u in range(CHUNK):
            t = g * CHUNK + u
            row, col = rows[t], cols[t]
            high, low = split(buf[t])
            p = dot(left_s[col], jnp.concatenate([high, low], 1), NT)
            m = dot(left_t[row], jnp.concatenate([high, low], 0), NN)
            alive = t < live
            done.append((jnp.where(alive, row, 64), jnp.where(alive, col, 32), p[:16] + p[16:], m[:16] + m[16:]))
        for row, col, p, m in done:
            pot[row] = pot[row] + p
            mir[col] = mir[col] + m
        return carry

    groups = (live + CHUNK - 1) // CHUNK
    lax.fori_loop(0, groups, group, 0)

    def drain(k, carry):
        fetch(k).wait()
        return carry

    lax.fori_loop(groups, TILES // CHUNK, drain, 0)
    pot_out[...] = pot[0:64]
    quad = [jnp.zeros((16, 128), f32) for _ in range(4)]
    for i in range(64):
        quad[i % 4] = quad[i % 4] + target[i] * pot[i]
    quad = 2.0 * jnp.sum((quad[0] + quad[1]) + (quad[2] + quad[3]), axis=1, keepdims=True)
    lane = lax.broadcasted_iota(jnp.int32, (16, 128), 1)
    all_sums = sums[...] + jnp.where(lane == 3, quad, 0.0)
    for k in range(4):
        there = (y + k) % 4
        for i in range(4):
            keep[k, i] = mir[(there * 2 + core) * 4 + i]
            send[k, i] = mir[(there * 2 + 1 - core) * 4 + i]
        keep[k, 4] = all_sums
        send[k, 4] = all_sums


def tile_products(pos, count, rows, cols, target, pieces, sums, tiles):
    return pl.pallas_call(
        tiles_kernel,
        out_shape=(shape(64, 16, 128), shape(4, 5, 16, 128), shape(4, 5, 16, 128)),
        in_specs=[SMEM] * 4 + [VMEM] * 7 + [ANY],
        out_specs=(VMEM, VMEM, VMEM),
        scratch_shapes=[
            pltpu.VMEM((128, 128, 128), f32),
            pltpu.SemaphoreType.DMA((TILES // CHUNK,)),
            pltpu.VMEM((32, 32, 256), bf16),
            pltpu.VMEM((64, 32, 256), bf16),
            pltpu.VMEM((65, 16, 128), f32),
            pltpu.VMEM((33, 16, 128), f32),
        ],
        compiler_params=params(24),
        name="tile_products",
    )(pos, count, rows, cols, target, *pieces, sums, tiles)


def summed(i, q, hard, pots, s0, s1, s2, s3):
    parts = [pots[k, i] for k in range(16)] + [s0[i], s1[i], s2[i], s3[i], hard[i : i + 1] * q[i]]
    while len(parts) > 1:
        parts = [a + b for a, b in zip(parts[::2], parts[1::2])] + ([parts[-1]] if len(parts) % 2 else [])
    return parts[0]


def second_kernel(items, places, number, pay, drive, q, hard, pots, s0, s1, s2, s3,
                  q_copies, q_own, v_own, sums, left, total, acc):
    n = number[0]
    for i in range(4):
        v = summed(i, q, hard, pots, s0, s1, s2, s3)
        v_own[i] = v
        left[i, 0:32] = stacked(drive[i])
        left[i, 32:64] = stacked(v)
    total[...] = jnp.zeros_like(total)
    acc[...] = jnp.zeros_like(acc)

    def group(g, carry):
        done = []
        m = [None] * 4
        for u in range(GROUP):
            t = g * GROUP + u
            valid = t < n
            item = jnp.where(valid, items[t], 0)
            place = jnp.where(valid, places[t], 4)
            gain, lose, stiff = slot_rows(pay, item)
            gain = jnp.where(valid, gain, -1.0)
            lose = jnp.where(valid, lose, -1.0)
            matrix = ends_matrix(gain, lose)
            both = dot(left[jnp.minimum(place, 3)], matrix, NN)
            r = -(both[0:16] + both[16:32])
            w = (both[32:48] + both[48:64]) + stiff * r
            back = dot(stacked(w), matrix, NT)
            done.append((place, back[:16] + back[16:]))
            terms = (r * r, r * w, w * w, stiff * (w * w))
            m = [b if a is None else a + b for a, b in zip(m, terms)]
        for place, back in done:
            total[place] = total[place] + back
        for j in range(4):
            acc[j] = acc[j] + m[j]
        return carry

    lax.fori_loop(0, (n + GROUP - 1) // GROUP, group, 0)
    q_own[...] = total[0:4]
    for k in range(16):
        q_copies[k] = total[0:4]
    lane = lax.broadcasted_iota(jnp.int32, (16, 128), 1)
    diag = acc[3]
    for i in range(4):
        diag = diag + hard[i : i + 1] * (total[i] * total[i])
    out = jnp.zeros((16, 128), f32)
    for j, value in enumerate((acc[0], acc[1], acc[2], diag)):
        out = jnp.where(lane == j, jnp.sum(value, axis=1, keepdims=True), out)
    sums[...] = out


def second(items, places, number, pay, drive, q, hard, pots, pieces):
    return pl.pallas_call(
        second_kernel,
        out_shape=(shape(16, 4, 16, 128), shape(4, 16, 128), shape(4, 16, 128), shape(16, 128)),
        in_specs=[SMEM] * 3 + [VMEM] * 9,
        out_specs=(VMEM, VMEM, VMEM, VMEM),
        scratch_shapes=[
            pltpu.VMEM((4, 64, 128), bf16),
            pltpu.VMEM((5, 16, 128), f32),
            pltpu.VMEM((4, 16, 128), f32),
        ],
        compiler_params=params(16),
        name="second_charges",
    )(items, places, number, pay, drive, q, hard, pots, *pieces)


def third_kernel(drive, v, q, hard, pots, s0, s1, s2, s3, out, own):
    for i in range(4):
        own[i] = drive[i]
        own[4 + i] = v[i]
        own[8 + i] = summed(i, q, hard, pots, s0, s1, s2, s3)
    own[12] = (s0[4] + s1[4]) + (s2[4] + s3[4])
    for k in range(16):
        out[k] = own[...]


def third(drive, v, q, hard, pots, pieces):
    return pl.pallas_call(
        third_kernel,
        out_shape=shape(16, 13, 16, 128),
        in_specs=[VMEM] * 9,
        out_specs=VMEM,
        scratch_shapes=[pltpu.VMEM((13, 16, 128), f32)],
        compiler_params=params(16),
        name="potentials_out",
    )(drive, v, q, hard, pots, *pieces)


def last_kernel(pos, bonds, cells, count, pay, got, keep, send, out):
    n = count[0]
    core = pos[2]
    sums = got[0, 12]
    for k in range(1, 16):
        sums = sums + got[k, 12]
    m0, m1, m2, m3 = (sums[:, j : j + 1] for j in range(4))
    step0 = m0 / m1
    norm1 = m0 - 2.0 * step0 * m1 + step0 * step0 * m2
    ratio = norm1 / m0
    grow = 1.0 + ratio
    step1 = norm1 / (grow * grow * m1 - 2.0 * step0 * grow * m2 + step0 * step0 * m3)
    wide = lambda a: jnp.broadcast_to(a, (16, 128))
    sol_r, sol_w = wide(step0 + step1 * grow), wide(-step1 * step0)
    res_w, res_z = wide(-step0 - step1 * grow), wide(step1 * step0)
    out[...] = jnp.zeros_like(out)

    def group(g, carry):
        done = []
        for u in range(GROUP):
            t = g * GROUP + u
            valid = t < n
            s = jnp.where(valid, t, 0)
            cell, block = cells[s], bonds[s]
            k, i = cell // 4, cell % 4
            gain, lose = pay[pl.ds(s, 1), :], pay[pl.ds(32 + s, 1), :]
            stiff = pay[pl.ds(64 + s, 1), :]
            gain = jnp.where(valid, gain, -1.0)
            lose = jnp.where(valid, lose, -1.0)
            matrix = ends_matrix(gain, lose)
            left = jnp.concatenate([stacked(got[k, i]), stacked(got[k, 4 + i]), stacked(got[k, 8 + i])], 0)
            b = dot(left, matrix, NN)
            r = -(b[0:16] + b[16:32])
            w = (b[32:48] + b[48:64]) + stiff * r
            z = (b[64:80] + b[80:96]) + stiff * w
            away = jnp.where((block // 8) % 2 == core, 0, 1)
            done.append((away, block // 16, block % 8, sol_r * r + sol_w * w, r + res_w * w + res_z * z))
        for away, there, at, sol, res in done:
            out[away, there, at] = out[away, there, at] + sol
            out[away, there, 8 + at] = out[away, there, 8 + at] + res
        return carry

    lax.fori_loop(0, (n + GROUP - 1) // GROUP, group, 0)
    keep[...] = out[0]
    send[...] = out[1]


def last(pos, bonds, cells, count, pay, got):
    return pl.pallas_call(
        last_kernel,
        out_shape=(shape(4, 16, 16, 128), shape(4, 16, 16, 128)),
        in_specs=[SMEM] * 4 + [VMEM] * 2,
        out_specs=(VMEM, VMEM),
        scratch_shapes=[pltpu.VMEM((2, 4, 16, 16, 128), f32)],
        compiler_params=params(16),
        name="bond_outputs",
    )(pos, bonds, cells, count, pay, got)


def shift(values, axis, by):
    n = lax.axis_size(axis)
    return lax.ppermute(values, axis, [(i, (i + by) % n) for i in range(n)])


def across(values, axis):
    return lax.all_to_all(values, axis, 0, 0, tiled=True)


def gather(copies, own):
    target = across(copies.reshape(64, 16, 128), ROW)
    near = shift(own, "core", 1)
    pair = jnp.concatenate([own, near], 0)
    return target, (own, near, *(shift(pair, "y", k) for k in (1, 2, 3)))


def scatter(pot, keep, send):
    got = across(pot, ROW).reshape(16, 4, 16, 128)
    total = keep + shift(send, "core", 1)
    return got, (total[0], *(shift(total[k], "y", k) for k in (1, 2, 3)))


def on_device(
    charge_drive,
    hardness,
    bond_stiffness,
    coulomb_tiles,
    tile_rows,
    tile_cols,
    tile_count,
    link_bonds,
    link_cells,
    link_ends,
    link_carry,
    link_count,
):
    row = lax.axis_index("x") * 4 + lax.axis_index("z")
    pos = jnp.stack([row, lax.axis_index("y"), lax.axis_index("core")]).astype(jnp.int32)
    copies, own_links = pack(
        link_bonds, link_count, link_cells.reshape(1, 32), link_ends, link_carry, bond_stiffness
    )
    pay = across(copies, ROW)
    meta = pay[:, META, :33].astype(jnp.int32).reshape(16 * 33)
    items, places, number, q_copies, q0 = first(pos, meta, pay, charge_drive)
    target, pieces = gather(q_copies, q0)
    zeros = jnp.zeros((16, 128), f32)
    pots, parts = scatter(
        *tile_products(pos, tile_count, tile_rows, tile_cols, target, pieces, zeros, coulomb_tiles)
    )
    q_copies, q1, v0, sums = second(items, places, number, pay, charge_drive, q0, hardness, pots, parts)
    target, pieces = gather(q_copies, q1)
    pots, parts = scatter(
        *tile_products(pos, tile_count, tile_rows, tile_cols, target, pieces, sums, coulomb_tiles)
    )
    copies = third(charge_drive, v0, q1, hardness, pots, parts)
    got = across(copies, ROW)
    keep, send = last(pos, link_bonds, link_cells, link_count, own_links, got)
    total = keep + shift(send, "core", 1)
    total = jnp.sum(across(total, "y"), axis=0)
    return total[:8], total[8:]


def solution(mesh):
    wide = Mesh(mesh.devices.reshape(4, 4, 4, 2), ALL)
    return jax.shard_map(
        on_device,
        mesh=wide,
        in_specs=(
            P(ALL, None, None),
            P(ALL, None),
            P(ROW, None),
            P(ALL, None, None),
            P(ALL),
            P(ALL),
            P(ALL),
            P(ALL),
            P(ALL),
            P(ALL, None, None),
            P(ALL, None),
            P(ALL),
        ),
        out_specs=(P(ALL, None, None), P(ALL, None, None)),
        check_vma=False,
    )
```

```python
import jax
import jax.numpy as jnp
from jax import lax
from jax.experimental import pallas as pl
from jax.experimental.pallas import tpu as pltpu
from jax.sharding import Mesh, PartitionSpec as P

f32 = jnp.float32
bf16 = jnp.bfloat16
ROW = ("x", "z")
ALL = ("x", "z", "y", "core")
NN = (((1,), (0,)), ((), ()))
NT = (((1,), (1,)), ((), ()))
SMEM = pl.BlockSpec(memory_space=pltpu.SMEM)
VMEM = pl.BlockSpec(memory_space=pltpu.VMEM)
HBM = pl.BlockSpec(memory_space=pltpu.HBM)
META = 96
PAY = 104
SPACE = 2 * 128


def shape(*dims):
    return jax.ShapeDtypeStruct(dims, f32)


def params(mib):
    return pltpu.CompilerParams(vmem_limit_bytes=mib << 20)


def split(values):
    high = values.astype(bf16)
    return high, (values - high.astype(f32)).astype(bf16)


def stacked(values):
    high, low = split(values)
    return jnp.concatenate([high, low], 0)


def dot(a, b, dims):
    return lax.dot_general(a, b, dims, preferred_element_type=f32)


def ends_matrix(gain, lose):
    atoms = lax.broadcasted_iota(jnp.int32, (128, 128), 0).astype(f32)
    one, zero = f32(1.0), f32(0.0)
    return (jnp.where(atoms == gain, one, zero) - jnp.where(atoms == lose, one, zero)).astype(bf16)


def started(*pairs_and_sems):
    copies = [pltpu.make_async_copy(*each) for each in pairs_and_sems]
    for copy in copies:
        copy.start()
    return copies


def pack_kernel(count_in, cells_in, bonds_in, ends_in, carry_in, stiff_in,
                out, order, own, count, cells, bonds, ends, carry, stiff, begin, sems):
    copies = started(
        (count_in, count, sems.at[0]),
        (cells_in, cells, sems.at[1]),
        (bonds_in, bonds, sems.at[2]),
        (ends_in, ends, sems.at[3]),
        (carry_in, carry, sems.at[4]),
        (stiff_in, stiff, sems.at[5]),
    )
    for copy in copies:
        copy.wait()
    live = count[0]
    owners = [jnp.where(s < live, cells[s] // 4, 16) for s in range(32)]
    for k in range(18):
        begin[k] = 0
    for owner in owners:
        begin[owner + 1] = begin[owner + 1] + 1
    for k in range(1, 18):
        begin[k] = begin[k] + begin[k - 1]
    firsts = [begin[k] for k in range(17)]
    slot = lax.broadcasted_iota(jnp.int32, (32, 128), 0)
    carried = (carry[...] > 0) & (slot < live)
    gain = jnp.where(carried, ends[:, 0, :].astype(f32), -1.0)
    lose = jnp.where(carried, ends[:, 1, :].astype(f32), -1.0)
    lane = lax.broadcasted_iota(jnp.int32, (8, 128), 1)
    named = jnp.zeros((8, 128), jnp.int32)
    for s in range(32):
        to = begin[owners[s]]
        begin[owners[s]] = to + 1
        order[to] = s
        own[pl.ds(to, 1), :] = gain[s : s + 1]
        own[pl.ds(32 + to, 1), :] = lose[s : s + 1]
        own[pl.ds(64 + to, 1), :] = stiff[pl.ds(bonds[s], 1), :]
        named = jnp.where(lane == 32 + to, cells[s] % 4, named)
    for k in range(16):
        out[k, 0:META] = own[...]
        row = jnp.where(lane == 0, firsts[k], jnp.where(lane == 1, firsts[k + 1] - firsts[k], named))
        out[k, META:PAY] = row.astype(f32)


def pack(count, cells, bonds, ends, carry, stiff):
    return pl.pallas_call(
        pack_kernel,
        out_shape=(shape(16, PAY, 128), jax.ShapeDtypeStruct((32,), jnp.int32)),
        in_specs=[HBM] * 6,
        out_specs=(VMEM, SMEM),
        scratch_shapes=[
            pltpu.VMEM((META, 128), f32),
            pltpu.SMEM((1,), jnp.int32),
            pltpu.SMEM((32,), jnp.int32),
            pltpu.SMEM((32,), jnp.int32),
            pltpu.VMEM((32, 2, 128), jnp.int32),
            pltpu.VMEM((32, 128), jnp.int32),
            pltpu.VMEM((64, 128), f32),
            pltpu.SMEM((32,), jnp.int32),
            pltpu.SemaphoreType.DMA((6,)),
        ],
        compiler_params=params(56),
        name="pack_links",
    )(count, cells, bonds, ends, carry, stiff)


CHUNK = 16
TILES = 128
CHUNKS = TILES // CHUNK


def halves_kernel(tiles, *refs):
    smalls, outs = refs[0:SMALLS], refs[SMALLS + 1 : 2 * SMALLS + 1]
    after, (out, whole, halved, in_sems, out_sems, sems) = refs[SMALLS], refs[2 * SMALLS + 1 :]

    def fetch(k):
        part = pl.ds(k * CHUNK, CHUNK)
        return pltpu.make_async_copy(tiles.at[part], whole.at[part], in_sems.at[k])

    def give(k):
        part = pl.ds(k * CHUNK, CHUNK)
        return pltpu.make_async_copy(halved.at[part], out.at[part], out_sems.at[k])

    for k in range(CHUNKS):
        fetch(k).start()
    copies = started(*((a, b, sems.at[j]) for j, (a, b) in enumerate(zip(smalls, outs))))

    def step(k, carry):
        fetch(k).wait()
        for u in range(CHUNK):
            high, low = split(whole[k * CHUNK + u])
            halved[k * CHUNK + u, 0:128] = high
            halved[k * CHUNK + u, 128:256] = low
        give(k).start()
        return carry

    lax.fori_loop(0, CHUNKS, step, 0)
    for k in range(CHUNKS):
        give(k).wait()
    for copy in copies:
        copy.wait()


SMALLS = 8


def halves(tiles, smalls, after):
    return pl.pallas_call(
        halves_kernel,
        out_shape=(
            *(jax.ShapeDtypeStruct(each.shape, each.dtype) for each in smalls),
            jax.ShapeDtypeStruct((SPACE, 256, 128), bf16),
        ),
        in_specs=[HBM] * (SMALLS + 1) + [SMEM],
        out_specs=(VMEM, VMEM, *[SMEM] * (SMALLS - 2), HBM),
        scratch_shapes=[
            pltpu.VMEM((TILES, 128, 128), f32),
            pltpu.VMEM((TILES, 256, 128), bf16),
            pltpu.SemaphoreType.DMA((CHUNKS,)),
            pltpu.SemaphoreType.DMA((CHUNKS,)),
            pltpu.SemaphoreType.DMA((SMALLS,)),
        ],
        cost_estimate=pl.CostEstimate(flops=3 << 21, bytes_accessed=16 << 20, transcendentals=0),
        compiler_params=params(52),
        name="tile_halves",
    )(tiles, *smalls, after)


def slot_rows(pay, item):
    k, s = item // 32, item % 32
    return k, s, pay[k, pl.ds(s, 1), :], pay[k, pl.ds(32 + s, 1), :]


GROUP = 8


def first_kernel(meta, pay, drive, items, places, number, q_copies, q_own, left, total):

    def from_sender(k, n):
        begin = meta[k * 64]

        def slot(j, n):
            items[n] = k * 32 + begin + j
            places[n] = meta[k * 64 + 32 + begin + j]
            return n + 1

        return lax.fori_loop(0, meta[k * 64 + 1], slot, n)

    n = lax.fori_loop(0, 16, from_sender, 0)
    number[0] = n
    for i in range(4):
        left[i] = stacked(drive[i])
    total[...] = jnp.zeros_like(total)

    def group(g, carry):
        done = []
        for u in range(GROUP):
            t = g * GROUP + u
            valid = t < n
            item = jnp.where(valid, items[t], 0)
            place = jnp.where(valid, places[t], 4)
            _, _, gain, lose = slot_rows(pay, item)
            matrix = ends_matrix(gain, lose)
            u2 = dot(left[jnp.minimum(place, 3)], matrix, NN)
            back = dot(stacked(-(u2[:16] + u2[16:])), matrix, NT)
            done.append((place, back[:16] + back[16:]))
        for place, back in done:
            total[place] = total[place] + back
        return carry

    lax.fori_loop(0, (n + GROUP - 1) // GROUP, group, 0)
    q_own[...] = total[0:4]
    for k in range(16):
        q_copies[k, 0:4] = total[0:4]
        q_copies[k, 4:6] = drive[0:2]


def first(meta, pay, drive):
    return pl.pallas_call(
        first_kernel,
        out_shape=(
            jax.ShapeDtypeStruct((520,), jnp.int32),
            jax.ShapeDtypeStruct((520,), jnp.int32),
            jax.ShapeDtypeStruct((1,), jnp.int32),
            shape(16, 6, 16, 128),
            shape(4, 16, 128),
        ),
        in_specs=[SMEM, VMEM, VMEM],
        out_specs=(SMEM, SMEM, SMEM, VMEM, VMEM),
        scratch_shapes=[
            pltpu.VMEM((4, 32, 128), bf16),
            pltpu.VMEM((5, 16, 128), f32),
        ],
        compiler_params=params(16),
        name="first_charges",
    )(meta, pay, drive)


def tiles_kernel(pos, count, rows, cols, target, own, y1, y2, y3, n0, n1, n2, n3, sums, ride, halved,
                 pot_out, keep, send, rode, tiles, sems, left_s, left_t, pot, mir):
    def fetch(k):
        part = pl.ds(k * CHUNK, CHUNK)
        return pltpu.make_async_copy(halved.at[part], tiles.at[part], sems.at[k])

    for k in range(CHUNKS):
        fetch(k).start()
    rode[...] = target[:, 4:6]
    y, core = pos[1], pos[2]

    def put(ref, at, values):
        high, low = split(values)
        ref[at, 0:16, 0:128] = high
        ref[at, 16:32, 0:128] = low
        ref[at, 0:16, 128:256] = high
        ref[at, 16:32, 128:256] = jnp.zeros_like(low)

    for i in range(64):
        put(left_t, i, target[i // 4, i % 4])
    for k, (mine, other) in enumerate(((own, n0), (y1, n1), (y2, n2), (y3, n3))):
        there = (y + 4 - k) % 4
        for i in range(4):
            put(left_s, (there * 2 + core) * 4 + i, mine[i])
            put(left_s, (there * 2 + 1 - core) * 4 + i, other[i])
    pot[...] = jnp.zeros_like(pot)
    mir[...] = jnp.zeros_like(mir)
    live = count[0]

    def group(g, carry):
        fetch(g).wait()
        done = []
        for u in range(CHUNK):
            t = g * CHUNK + u
            row, col = rows[t], cols[t]
            high, low = tiles[t, 0:128], tiles[t, 128:256]
            p = dot(left_s[col], jnp.concatenate([high.T, low.T], 0), NN)
            m = dot(left_t[row], tiles[t], NN)
            alive = t < live
            done.append((jnp.where(alive, row, 64), jnp.where(alive, col, 32), p[:16] + p[16:], m[:16] + m[16:]))
        for row, col, p, m in done:
            pot[row] = pot[row] + p
            mir[col] = mir[col] + m
        return carry

    def drain(k, carry):
        fetch(k).wait()
        return carry

    groups = (live + CHUNK - 1) // CHUNK
    lax.fori_loop(0, groups, group, 0)
    lax.fori_loop(groups, CHUNKS, drain, 0)
    for k in range(16):
        pot_out[k, 0:4] = pot[4 * k : 4 * k + 4]
        pot_out[k, 4:6] = ride[2:4]
    quad = [jnp.zeros((16, 128), f32) for _ in range(4)]
    for i in range(64):
        quad[i % 4] = quad[i % 4] + target[i // 4, i % 4] * pot[i]
    quad = 2.0 * jnp.sum((quad[0] + quad[1]) + (quad[2] + quad[3]), axis=1, keepdims=True)
    lane = lax.broadcasted_iota(jnp.int32, (16, 128), 1)
    all_sums = sums[...] + jnp.where(lane == 3, quad, 0.0)
    for k in range(4):
        there = (y + k) % 4
        for i in range(4):
            keep[k, i] = mir[(there * 2 + core) * 4 + i]
            send[k, i] = mir[(there * 2 + 1 - core) * 4 + i]
        keep[k, 4] = all_sums
        send[k, 4] = all_sums


def tile_products(pos, count, rows, cols, target, pieces, sums, ride, tiles):
    return pl.pallas_call(
        tiles_kernel,
        out_shape=(shape(16, 6, 16, 128), shape(4, 5, 16, 128), shape(4, 5, 16, 128), shape(16, 2, 16, 128)),
        in_specs=[SMEM] * 4 + [VMEM] * 11 + [HBM],
        out_specs=(VMEM, VMEM, VMEM, VMEM),
        scratch_shapes=[
            pltpu.VMEM((TILES, 256, 128), bf16),
            pltpu.SemaphoreType.DMA((CHUNKS,)),
            pltpu.VMEM((32, 32, 256), bf16),
            pltpu.VMEM((64, 32, 256), bf16),
            pltpu.VMEM((65, 16, 128), f32),
            pltpu.VMEM((33, 16, 128), f32),
        ],
        compiler_params=params(44),
        name="tile_products",
    )(pos, count, rows, cols, target, *pieces, sums, ride, tiles)


def summed(i, q, hard, pots, s0, s1, s2, s3):
    parts = [pots[k, i] for k in range(16)] + [s0[i], s1[i], s2[i], s3[i], hard[i : i + 1] * q[i]]
    while len(parts) > 1:
        parts = [a + b for a, b in zip(parts[::2], parts[1::2])] + ([parts[-1]] if len(parts) % 2 else [])
    return parts[0]


def second_kernel(items, places, number, pay, drive, q, hard, pots, s0, s1, s2, s3,
                  q_copies, q_own, v_own, sums, rode, left, total, acc):
    rode[...] = pots[:, 4:6]
    n = number[0]
    total[...] = jnp.zeros_like(total)
    acc[...] = jnp.zeros_like(acc)
    for i in range(4):
        v = summed(i, q, hard, pots, s0, s1, s2, s3)
        v_own[i] = v
        left[i, 0:32] = stacked(drive[i])
        left[i, 32:64] = stacked(v)

    def group(g, carry):
        done = []
        m = [None] * 4
        for u in range(GROUP):
            t = g * GROUP + u
            valid = t < n
            item = jnp.where(valid, items[t], 0)
            place = jnp.where(valid, places[t], 4)
            k, s, gain, lose = slot_rows(pay, item)
            stiff = pay[k, pl.ds(64 + s, 1), :]
            gain = jnp.where(valid, gain, -1.0)
            lose = jnp.where(valid, lose, -1.0)
            matrix = ends_matrix(gain, lose)
            both = dot(left[jnp.minimum(place, 3)], matrix, NN)
            r = -(both[0:16] + both[16:32])
            w = (both[32:48] + both[48:64]) + stiff * r
            back = dot(stacked(w), matrix, NT)
            done.append((place, back[:16] + back[16:]))
            terms = (r * r, r * w, w * w, stiff * (w * w))
            m = [b if a is None else a + b for a, b in zip(m, terms)]
        for place, back in done:
            total[place] = total[place] + back
        for j in range(4):
            acc[j] = acc[j] + m[j]
        return carry

    lax.fori_loop(0, (n + GROUP - 1) // GROUP, group, 0)
    q_own[...] = total[0:4]
    for k in range(16):
        q_copies[k, 0:4] = total[0:4]
        q_copies[k, 4:6] = v_own[0:2]
    lane = lax.broadcasted_iota(jnp.int32, (16, 128), 1)
    diag = acc[3]
    for i in range(4):
        diag = diag + hard[i : i + 1] * (total[i] * total[i])
    out = jnp.zeros((16, 128), f32)
    for j, value in enumerate((acc[0], acc[1], acc[2], diag)):
        out = jnp.where(lane == j, jnp.sum(value, axis=1, keepdims=True), out)
    sums[...] = out


def second(items, places, number, pay, drive, q, hard, pots, pieces):
    return pl.pallas_call(
        second_kernel,
        out_shape=(
            shape(16, 6, 16, 128),
            shape(4, 16, 128),
            shape(4, 16, 128),
            shape(16, 128),
            shape(16, 2, 16, 128),
        ),
        in_specs=[SMEM] * 3 + [VMEM] * 9,
        out_specs=(VMEM,) * 5,
        scratch_shapes=[
            pltpu.VMEM((4, 64, 128), bf16),
            pltpu.VMEM((5, 16, 128), f32),
            pltpu.VMEM((4, 16, 128), f32),
        ],
        compiler_params=params(16),
        name="second_charges",
    )(items, places, number, pay, drive, q, hard, pots, *pieces)


def third_kernel(q, hard, pots, s0, s1, s2, s3, out, rode):
    rode[...] = pots[:, 4:6]
    sums = (s0[4] + s1[4]) + (s2[4] + s3[4])
    for k in range(16):
        out[k, 4] = sums
    for i in range(4):
        v = summed(i, q, hard, pots, s0, s1, s2, s3)
        for k in range(16):
            out[k, i] = v


def third(q, hard, pots, pieces):
    return pl.pallas_call(
        third_kernel,
        out_shape=(shape(16, 5, 16, 128), shape(16, 2, 16, 128)),
        in_specs=[VMEM] * 7,
        out_specs=(VMEM, VMEM),
        compiler_params=params(16),
        name="potentials_out",
    )(q, hard, pots, *pieces)


def last_kernel(pos, bonds, cells, count, order, pay, a0, a1, b0, b1, got, keep, send, out, held):
    n = count[0]
    row, core = pos[0], pos[2]
    sums = got[0, 4]
    for k in range(1, 16):
        sums = sums + got[k, 4]
    m0, m1, m2, m3 = (sums[:, j : j + 1] for j in range(4))
    step0 = m0 / m1
    norm1 = m0 - 2.0 * step0 * m1 + step0 * step0 * m2
    ratio = norm1 / m0
    grow = 1.0 + ratio
    step1 = norm1 / (grow * grow * m1 - 2.0 * step0 * grow * m2 + step0 * step0 * m3)
    wide = lambda a: jnp.broadcast_to(a, (16, 128))
    sol_r, sol_w = wide(step0 + step1 * grow), wide(-step1 * step0)
    res_w, res_z = wide(-step0 - step1 * grow), wide(step1 * step0)
    out[...] = jnp.zeros_like(out)
    for j, parts in enumerate(((a0, a1), (b0, b1))):
        held[j, :, 0:2] = parts[0][...]
        held[j, :, 2:4] = parts[1][...]

    def group(g, carry):
        done = []
        for u in range(GROUP):
            t = g * GROUP + u
            valid = t < n
            s = jnp.where(valid, t, 0)
            cell, block = cells[order[s]], bonds[order[s]]
            k, i = cell // 4, cell % 4
            gain, lose = pay[row, pl.ds(s, 1), :], pay[row, pl.ds(32 + s, 1), :]
            stiff = pay[row, pl.ds(64 + s, 1), :]
            gain = jnp.where(valid, gain, -1.0)
            lose = jnp.where(valid, lose, -1.0)
            matrix = ends_matrix(gain, lose)
            left = jnp.concatenate([stacked(held[0, k, i]), stacked(held[1, k, i]), stacked(got[k, i])], 0)
            b = dot(left, matrix, NN)
            r = -(b[0:16] + b[16:32])
            w = (b[32:48] + b[48:64]) + stiff * r
            z = (b[64:80] + b[80:96]) + stiff * w
            away = jnp.where((block // 8) % 2 == core, 0, 1)
            done.append((away, (block // 16 + 4 - pos[1]) % 4, block % 8, sol_r * r + sol_w * w, r + res_w * w + res_z * z))
        for away, there, at, sol, res in done:
            out[away, there, at] = out[away, there, at] + sol
            out[away, there, 8 + at] = out[away, there, 8 + at] + res
        return carry

    lax.fori_loop(0, (n + GROUP - 1) // GROUP, group, 0)
    keep[...] = out[0]
    send[...] = out[1]


def last(pos, bonds, cells, count, order, pay, rides, got):
    return pl.pallas_call(
        last_kernel,
        out_shape=(shape(4, 16, 16, 128), shape(4, 16, 16, 128)),
        in_specs=[SMEM] * 5 + [VMEM] * 6,
        out_specs=(VMEM, VMEM),
        scratch_shapes=[pltpu.VMEM((2, 4, 16, 16, 128), f32), pltpu.VMEM((2, 16, 4, 16, 128), f32)],
        compiler_params=params(16),
        name="bond_outputs",
    )(pos, bonds, cells, count, order, pay, *rides, got)


def shift(values, axis, by):
    n = lax.axis_size(axis)
    return lax.ppermute(values, axis, [(i, (i + by) % n) for i in range(n)])


def across(values, axis):
    return lax.all_to_all(values, axis, 0, 0, tiled=True)


def gather(copies, own):
    target = across(copies, ROW)
    mine = (own, *(shift(own, "y", k) for k in (1, 2, 3)))
    return target, (*mine, *(shift(each, "core", 1) for each in mine))


def scatter(pot, keep, send):
    got = across(pot, ROW)
    total = keep + shift(send, "core", 1)
    return got, (total[0], *(shift(total[k], "y", k) for k in (1, 2, 3)))


def on_device(
    charge_drive,
    hardness,
    bond_stiffness,
    coulomb_tiles,
    tile_rows,
    tile_cols,
    tile_count,
    link_bonds,
    link_cells,
    link_ends,
    link_carry,
    link_count,
):
    row = lax.axis_index("x") * 4 + lax.axis_index("z")
    pos = jnp.stack([row, lax.axis_index("y"), lax.axis_index("core")]).astype(jnp.int32)
    links, order = pack(link_count, link_cells, link_bonds, link_ends, link_carry, bond_stiffness)
    pay = across(links, ROW)
    smalls = (charge_drive, hardness, tile_count, tile_rows, tile_cols, link_bonds, link_cells, link_count)
    drive, hard, tile_count, tile_rows, tile_cols, link_bonds, link_cells, link_count, tiles = halves(
        coulomb_tiles, smalls, order
    )
    meta = pay[:, META, :64].astype(jnp.int32).reshape(16 * 64)
    items, places, number, q_copies, q0 = first(meta, pay, drive)
    maps = (pos, tile_count, tile_rows, tile_cols)
    target, pieces = gather(q_copies, q0)
    zeros = jnp.zeros((16, 128), f32)
    *partial, ride0 = tile_products(*maps, target, pieces, zeros, drive, tiles)
    pots, parts = scatter(*partial)
    q_copies, q1, v0, sums, ride1 = second(items, places, number, pay, drive, q0, hard, pots, parts)
    target, pieces = gather(q_copies, q1)
    *partial, ride2 = tile_products(*maps, target, pieces, sums, v0, tiles)
    pots, parts = scatter(*partial)
    copies, ride3 = third(q1, hard, pots, parts)
    got = across(copies, ROW)
    rides = (ride0, ride1, ride2, ride3)
    keep, send = last(pos, link_bonds, link_cells, link_count, order, pay, rides, got)
    total = keep + shift(send, "core", 1)
    total = total[0] + shift(total[1], "y", 1) + shift(total[2], "y", 2) + shift(total[3], "y", 3)
    return total[:8], total[8:]


def solution(mesh):
    wide = Mesh(mesh.devices.reshape(4, 4, 4, 2), ALL)
    return jax.shard_map(
        on_device,
        mesh=wide,
        in_specs=(
            P(ALL, None, None),
            P(ALL, None),
            P(ROW, None),
            P(ALL, None, None),
            P(ALL),
            P(ALL),
            P(ALL),
            P(ALL),
            P(ALL),
            P(ALL, None, None),
            P(ALL, None),
            P(ALL),
        ),
        out_specs=(P(ALL, None, None), P(ALL, None, None)),
        check_vma=False,
    )
```

```python
import functools

import jax
import jax.numpy as jnp
from jax import lax
from jax.experimental import pallas as pl
from jax.experimental.pallas import tpu as pltpu
from jax.sharding import Mesh, PartitionSpec as P

f32 = jnp.float32
bf16 = jnp.bfloat16
ROW = ("x", "z")
ALL = ("x", "z", "y", "core")
NN = (((1,), (0,)), ((), ()))
NT = (((1,), (1,)), ((), ()))
SMEM = pl.BlockSpec(memory_space=pltpu.SMEM)
VMEM = pl.BlockSpec(memory_space=pltpu.VMEM)
HBM = pl.BlockSpec(memory_space=pltpu.HBM)
META = 64
PAY = 88
SPACE = 2 * 128


def shape(*dims):
    return jax.ShapeDtypeStruct(dims, f32)


def params(mib):
    return pltpu.CompilerParams(vmem_limit_bytes=mib << 20)


def split(values):
    high = values.astype(bf16)
    return high, (values - high.astype(f32)).astype(bf16)


def stacked(values):
    high, low = split(values)
    return jnp.concatenate([high, low], 0)


def dot(a, b, dims):
    return lax.dot_general(a, b, dims, preferred_element_type=f32)


def ends_matrix(gain, lose):
    atoms = lax.broadcasted_iota(jnp.int32, (128, 128), 0).astype(f32)
    one, zero = f32(1.0), f32(0.0)
    return (jnp.where(atoms == gain, one, zero) - jnp.where(atoms == lose, one, zero)).astype(bf16)


def started(*pairs_and_sems):
    copies = [pltpu.make_async_copy(*each) for each in pairs_and_sems]
    for copy in copies:
        copy.start()
    return copies


def pack_kernel(count_in, cells_in, bonds_in, ends_in, carry_in, stiff_in, drive_in,
                out, stiffs, order, own, count, cells, bonds, ends, carry, stiff, drive, begin, sems):
    copies = started(
        (count_in, count, sems.at[0]),
        (cells_in, cells, sems.at[1]),
        (bonds_in, bonds, sems.at[2]),
        (ends_in, ends, sems.at[3]),
        (carry_in, carry, sems.at[4]),
        (stiff_in, stiff, sems.at[5]),
        (drive_in.at[0], drive, sems.at[6]),
    )
    for copy in copies:
        copy.wait()
    live = count[0]
    owners = [jnp.where(s < live, cells[s] // 4, 16) for s in range(32)]
    for k in range(18):
        begin[k] = 0
    for owner in owners:
        begin[owner + 1] = begin[owner + 1] + 1
    for k in range(1, 18):
        begin[k] = begin[k] + begin[k - 1]
    firsts = [begin[k] for k in range(17)]
    slot = lax.broadcasted_iota(jnp.int32, (32, 128), 0)
    carried = (carry[...] > 0) & (slot < live)
    gain = jnp.where(carried, ends[:, 0, :].astype(f32), -1.0)
    lose = jnp.where(carried, ends[:, 1, :].astype(f32), -1.0)
    lane = lax.broadcasted_iota(jnp.int32, (8, 128), 1)
    named = jnp.zeros((8, 128), jnp.int32)
    for s in range(32):
        to = begin[owners[s]]
        begin[owners[s]] = to + 1
        order[to] = s
        own[pl.ds(to, 1), :] = gain[s : s + 1]
        own[pl.ds(32 + to, 1), :] = lose[s : s + 1]
        stiffs[pl.ds(to, 1), :] = stiff[pl.ds(bonds[s], 1), :]
        named = jnp.where(lane == 32 + to, cells[s] % 4, named)
    for k in range(16):
        out[k, 0:META] = own[...]
        row = jnp.where(lane == 0, firsts[k], jnp.where(lane == 1, firsts[k + 1] - firsts[k], named))
        out[k, META : META + 8] = row.astype(f32)
        out[k, META + 8 : PAY] = drive[...]


def pack(count, cells, bonds, ends, carry, stiff, drive):
    return pl.pallas_call(
        pack_kernel,
        out_shape=(shape(16, PAY, 128), shape(32, 128), jax.ShapeDtypeStruct((32,), jnp.int32)),
        in_specs=[HBM] * 7,
        out_specs=(VMEM, VMEM, SMEM),
        scratch_shapes=[
            pltpu.VMEM((META, 128), f32),
            pltpu.SMEM((1,), jnp.int32),
            pltpu.SMEM((32,), jnp.int32),
            pltpu.SMEM((32,), jnp.int32),
            pltpu.VMEM((32, 2, 128), jnp.int32),
            pltpu.VMEM((32, 128), jnp.int32),
            pltpu.VMEM((64, 128), f32),
            pltpu.VMEM((16, 128), f32),
            pltpu.SMEM((32,), jnp.int32),
            pltpu.SemaphoreType.DMA((7,)),
        ],
        compiler_params=params(56),
        name="pack_links",
    )(count, cells, bonds, ends, carry, stiff, drive)


CHUNK = 16
TILES = 128
CHUNKS = TILES // CHUNK
BONDS, CELLS, ORDER, LIVE_TILES, LIVE_LINKS = 256, 288, 320, 352, 353


def halves_kernel(tiles, drive, hard, stiffs, drive_out, hard_out, stiffs_out, out, whole, halved, in_sems, out_sems):

    def fetch(k):
        part = pl.ds(k * CHUNK, CHUNK)
        return pltpu.make_async_copy(tiles.at[part], whole.at[part], in_sems.at[k])

    def give(k):
        part = pl.ds(k * CHUNK, CHUNK)
        return pltpu.make_async_copy(halved.at[part], out.at[part], out_sems.at[k])

    for k in range(CHUNKS):
        fetch(k).start()
    drive_out[...] = drive[...]
    hard_out[...] = hard[...]
    stiffs_out[...] = stiffs[...]

    def step(k, carry):
        fetch(k).wait()
        for u in range(CHUNK):
            high, low = split(whole[k * CHUNK + u])
            halved[k * CHUNK + u, 0:128] = high
            halved[k * CHUNK + u, 128:256] = low
        give(k).start()
        return carry

    lax.fori_loop(0, CHUNKS, step, 0)
    for k in range(CHUNKS):
        give(k).wait()


def halves(tiles, drive, hard, stiffs):
    return pl.pallas_call(
        halves_kernel,
        out_shape=(
            shape(4, 16, 128),
            shape(4, 128),
            shape(32, 128),
            jax.ShapeDtypeStruct((SPACE, 256, 128), bf16),
        ),
        in_specs=[HBM, VMEM, VMEM, VMEM],
        out_specs=(VMEM, VMEM, VMEM, HBM),
        scratch_shapes=[
            pltpu.VMEM((TILES, 128, 128), f32),
            pltpu.VMEM((TILES, 256, 128), bf16),
            pltpu.SemaphoreType.DMA((CHUNKS,)),
            pltpu.SemaphoreType.DMA((CHUNKS,)),
        ],
        cost_estimate=pl.CostEstimate(flops=3 << 21, bytes_accessed=16 << 20, transcendentals=0),
        compiler_params=params(52),
        name="tile_halves",
    )(tiles, drive, hard, stiffs)


def slot_rows(pay, item):
    k, s = item // 32, item % 32
    return k, s, pay[k, pl.ds(s, 1), :], pay[k, pl.ds(32 + s, 1), :]


GROUP = 16
LAST_GROUP = 8


def first_kernel(meta, pay, drive, stiffs, items, places, number, q_copies, q_own, left, total):

    def from_sender(k, n):
        begin = meta[k * 64]

        def slot(j, n):
            items[n] = k * 32 + begin + j
            places[n] = meta[k * 64 + 32 + begin + j]
            return n + 1

        return lax.fori_loop(0, meta[k * 64 + 1], slot, n)

    n = lax.fori_loop(0, 16, from_sender, 0)
    number[0] = n
    for i in range(4):
        left[i] = stacked(drive[i])
    total[...] = jnp.zeros_like(total)

    def group(g, carry):
        done = []
        for u in range(GROUP):
            t = g * GROUP + u
            valid = t < n
            item = jnp.where(valid, items[t], 0)
            place = jnp.where(valid, places[t], 4)
            _, _, gain, lose = slot_rows(pay, item)
            matrix = ends_matrix(gain, lose)
            u2 = dot(left[jnp.minimum(place, 3)], matrix, NN)
            back = dot(stacked(-(u2[:16] + u2[16:])), matrix, NT)
            done.append((place, back[:16] + back[16:]))
        for place, back in done:
            total[place] = total[place] + back
        return carry

    lax.fori_loop(0, (n + GROUP - 1) // GROUP, group, 0)
    q_own[...] = total[0:4]
    for k in range(16):
        q_copies[k, 0:4] = total[0:4]
        q_copies[k, 4] = stiffs[0:16]
        q_copies[k, 5] = stiffs[16:32]


def first(meta, pay, drive, stiffs):
    return pl.pallas_call(
        first_kernel,
        out_shape=(
            jax.ShapeDtypeStruct((520,), jnp.int32),
            jax.ShapeDtypeStruct((520,), jnp.int32),
            jax.ShapeDtypeStruct((1,), jnp.int32),
            shape(16, 6, 16, 128),
            shape(4, 16, 128),
        ),
        in_specs=[SMEM, VMEM, VMEM, VMEM],
        out_specs=(SMEM, SMEM, SMEM, VMEM, VMEM),
        scratch_shapes=[
            pltpu.VMEM((4, 32, 128), bf16),
            pltpu.VMEM((5, 16, 128), f32),
        ],
        compiler_params=params(16),
        name="first_charges",
    )(meta, pay, drive, stiffs)


def tiles_kernel(begin, pos, ints, target, p0, p1, p2, p3, sums, ride, halved,
                 pot_out, keep, send, rode, tiles, sems, left_s, left_t, pot, mir):
    def fetch(k):
        part = pl.ds(k * CHUNK, CHUNK)
        return pltpu.make_async_copy(halved.at[part], tiles.at[part], sems.at[k])

    for k in range(CHUNKS):
        fetch(k).start()
    rode[...] = target[:, 4:6]
    y, core = pos[1], pos[2]

    def put(ref, at, values):
        high, low = split(values)
        ref[at, 0:16, 0:128] = high
        ref[at, 16:32, 0:128] = low
        ref[at, 0:16, 128:256] = high
        ref[at, 16:32, 128:256] = jnp.zeros_like(low)

    for i in range(64):
        put(left_t, i, target[i // 4, i % 4])
    for k, pair in enumerate((p0, p1, p2, p3)):
        there = (y + 4 - k) % 4
        for i in range(4):
            put(left_s, (there * 2 + core) * 4 + i, pair[i])
            put(left_s, (there * 2 + 1 - core) * 4 + i, pair[4 + i])
    pot[...] = jnp.zeros_like(pot)
    mir[...] = jnp.zeros_like(mir)
    live = ints[LIVE_TILES]

    def group(g, carry):
        fetch(g).wait()
        done = []
        for u in range(CHUNK):
            t = g * CHUNK + u
            row, col = ints[t], ints[TILES + t]
            high, low = tiles[t, 0:128], tiles[t, 128:256]
            p = dot(left_s[col], jnp.concatenate([high.T, low.T], 0), NN)
            m = dot(left_t[row], tiles[t], NN)
            alive = t < live
            done.append((jnp.where(alive, row, 64), jnp.where(alive, col, 32), p[:16] + p[16:], m[:16] + m[16:]))
        for row, col, p, m in done:
            pot[row] = pot[row] + p
            mir[col] = mir[col] + m
        return carry

    def drain(k, carry):
        fetch(k).wait()
        return carry

    groups = (live + CHUNK - 1) // CHUNK
    lax.fori_loop(0, groups, group, 0)
    lax.fori_loop(groups, CHUNKS, drain, 0)
    for k in range(16):
        pot_out[k, 0:4] = pot[4 * k : 4 * k + 4]
        pot_out[k, 4:6] = ride[begin : begin + 2]
    quad = [jnp.zeros((16, 128), f32) for _ in range(4)]
    for i in range(64):
        quad[i % 4] = quad[i % 4] + target[i // 4, i % 4] * pot[i]
    quad = 2.0 * jnp.sum((quad[0] + quad[1]) + (quad[2] + quad[3]), axis=1, keepdims=True)
    lane = lax.broadcasted_iota(jnp.int32, (16, 128), 1)
    all_sums = sums[...] + jnp.where(lane == 3, quad, 0.0)
    for k in range(4):
        there = (y + k) % 4
        for i in range(4):
            keep[k, i] = mir[(there * 2 + core) * 4 + i]
            send[k, i] = mir[(there * 2 + 1 - core) * 4 + i]
        keep[k, 4] = all_sums
        send[k, 4] = all_sums


def tile_products(begin, pos, ints, target, pieces, sums, ride, tiles):
    return pl.pallas_call(
        functools.partial(tiles_kernel, begin),
        out_shape=(shape(16, 6, 16, 128), shape(4, 5, 16, 128), shape(4, 5, 16, 128), shape(16, 2, 16, 128)),
        in_specs=[SMEM] * 2 + [VMEM] * 7 + [HBM],
        out_specs=(VMEM, VMEM, VMEM, VMEM),
        scratch_shapes=[
            pltpu.VMEM((TILES, 256, 128), bf16),
            pltpu.SemaphoreType.DMA((CHUNKS,)),
            pltpu.VMEM((32, 32, 256), bf16),
            pltpu.VMEM((64, 32, 256), bf16),
            pltpu.VMEM((65, 16, 128), f32),
            pltpu.VMEM((33, 16, 128), f32),
        ],
        compiler_params=params(44),
        name="tile_products",
    )(pos, ints, target, *pieces, sums, ride, tiles)


def summed(i, q, hard, pots, s0, s1, s2, s3):
    parts = [pots[k, i] for k in range(16)] + [s0[i], s1[i], s2[i], s3[i], hard[i : i + 1] * q[i]]
    while len(parts) > 1:
        parts = [a + b for a, b in zip(parts[::2], parts[1::2])] + ([parts[-1]] if len(parts) % 2 else [])
    return parts[0]


def second_kernel(items, places, number, pay, stiffs, drive, q, hard, pots, s0, s1, s2, s3,
                  q_copies, q_own, v_own, sums, rode, left, total, acc):
    rode[...] = pots[:, 4:6]
    n = number[0]
    total[...] = jnp.zeros_like(total)
    acc[...] = jnp.zeros_like(acc)
    for i in range(4):
        v = summed(i, q, hard, pots, s0, s1, s2, s3)
        v_own[i] = v
        left[i, 0:32] = stacked(drive[i])
        left[i, 32:64] = stacked(v)

    def group(g, carry):
        done = []
        m = [None] * 4
        for u in range(GROUP):
            t = g * GROUP + u
            valid = t < n
            item = jnp.where(valid, items[t], 0)
            place = jnp.where(valid, places[t], 4)
            k, s, gain, lose = slot_rows(pay, item)
            stiff = stiffs[k, pl.ds(s, 1), :]
            gain = jnp.where(valid, gain, -1.0)
            lose = jnp.where(valid, lose, -1.0)
            matrix = ends_matrix(gain, lose)
            both = dot(left[jnp.minimum(place, 3)], matrix, NN)
            r = -(both[0:16] + both[16:32])
            w = (both[32:48] + both[48:64]) + stiff * r
            back = dot(stacked(w), matrix, NT)
            done.append((place, back[:16] + back[16:]))
            terms = (r * r, r * w, w * w, stiff * (w * w))
            m = [b if a is None else a + b for a, b in zip(m, terms)]
        for place, back in done:
            total[place] = total[place] + back
        for j in range(4):
            acc[j] = acc[j] + m[j]
        return carry

    lax.fori_loop(0, (n + GROUP - 1) // GROUP, group, 0)
    q_own[...] = total[0:4]
    for k in range(16):
        q_copies[k, 0:4] = total[0:4]
        q_copies[k, 4:6] = v_own[0:2]
    lane = lax.broadcasted_iota(jnp.int32, (16, 128), 1)
    diag = acc[3]
    for i in range(4):
        diag = diag + hard[i : i + 1] * (total[i] * total[i])
    out = jnp.zeros((16, 128), f32)
    for j, value in enumerate((acc[0], acc[1], acc[2], diag)):
        out = jnp.where(lane == j, jnp.sum(value, axis=1, keepdims=True), out)
    sums[...] = out


def second(items, places, number, pay, stiffs, drive, q, hard, pots, pieces):
    return pl.pallas_call(
        second_kernel,
        out_shape=(
            shape(16, 6, 16, 128),
            shape(4, 16, 128),
            shape(4, 16, 128),
            shape(16, 128),
            shape(16, 2, 16, 128),
        ),
        in_specs=[SMEM] * 3 + [VMEM] * 10,
        out_specs=(VMEM,) * 5,
        scratch_shapes=[
            pltpu.VMEM((4, 64, 128), bf16),
            pltpu.VMEM((5, 16, 128), f32),
            pltpu.VMEM((4, 16, 128), f32),
        ],
        compiler_params=params(16),
        name="second_charges",
    )(items, places, number, pay, stiffs, drive, q, hard, pots, *pieces)


def third_kernel(drive, q, hard, pots, s0, s1, s2, s3, out, rode):
    rode[...] = pots[:, 4:6]
    sums = (s0[4] + s1[4]) + (s2[4] + s3[4])
    for k in range(16):
        out[k, 4] = sums
        out[k, 5] = drive[3]
    for i in range(4):
        v = summed(i, q, hard, pots, s0, s1, s2, s3)
        for k in range(16):
            out[k, i] = v


def third(drive, q, hard, pots, pieces):
    return pl.pallas_call(
        third_kernel,
        out_shape=(shape(16, 6, 16, 128), shape(16, 2, 16, 128)),
        in_specs=[VMEM] * 8,
        out_specs=(VMEM, VMEM),
        compiler_params=params(16),
        name="potentials_out",
    )(drive, q, hard, pots, *pieces)


def last_kernel(pos, ints, pay, stiffs, a1, b0, b1, got, keep, send, out, held):
    n = ints[LIVE_LINKS]
    row, core = pos[0], pos[2]
    sums = got[0, 4]
    for k in range(1, 16):
        sums = sums + got[k, 4]
    m0, m1, m2, m3 = (sums[:, j : j + 1] for j in range(4))
    step0 = m0 / m1
    norm1 = m0 - 2.0 * step0 * m1 + step0 * step0 * m2
    ratio = norm1 / m0
    grow = 1.0 + ratio
    step1 = norm1 / (grow * grow * m1 - 2.0 * step0 * grow * m2 + step0 * step0 * m3)
    wide = lambda a: jnp.broadcast_to(a, (16, 128))
    sol_r, sol_w = wide(step0 + step1 * grow), wide(-step1 * step0)
    res_w, res_z = wide(-step0 - step1 * grow), wide(step1 * step0)
    out[...] = jnp.zeros_like(out)
    for k in range(16):
        held[0, k, 0] = pay[k, META + 8 : PAY]
        held[0, k, 3] = got[k, 5]
    held[0, :, 1:3] = a1[...]
    held[1, :, 0:2] = b0[...]
    held[1, :, 2:4] = b1[...]

    def group(g, carry):
        done = []
        for u in range(LAST_GROUP):
            t = g * LAST_GROUP + u
            valid = t < n
            s = jnp.where(valid, t, 0)
            named = ints[ORDER + s]
            cell, block = ints[CELLS + named], ints[BONDS + named]
            k, i = cell // 4, cell % 4
            gain, lose = pay[row, pl.ds(s, 1), :], pay[row, pl.ds(32 + s, 1), :]
            stiff = stiffs[row, pl.ds(s, 1), :]
            gain = jnp.where(valid, gain, -1.0)
            lose = jnp.where(valid, lose, -1.0)
            matrix = ends_matrix(gain, lose)
            left = jnp.concatenate([stacked(held[0, k, i]), stacked(held[1, k, i]), stacked(got[k, i])], 0)
            b = dot(left, matrix, NN)
            r = -(b[0:16] + b[16:32])
            w = (b[32:48] + b[48:64]) + stiff * r
            z = (b[64:80] + b[80:96]) + stiff * w
            away = jnp.where((block // 8) % 2 == core, 0, 1)
            done.append((away, (block // 16 + 4 - pos[1]) % 4, block % 8, sol_r * r + sol_w * w, r + res_w * w + res_z * z))
        for away, there, at, sol, res in done:
            out[away, there, at] = out[away, there, at] + sol
            out[away, there, 8 + at] = out[away, there, 8 + at] + res
        return carry

    lax.fori_loop(0, (n + LAST_GROUP - 1) // LAST_GROUP, group, 0)
    keep[...] = out[0]
    send[...] = out[1]


def last(pos, ints, pay, rides, got):
    return pl.pallas_call(
        last_kernel,
        out_shape=(shape(4, 16, 16, 128), shape(4, 16, 16, 128)),
        in_specs=[SMEM] * 2 + [VMEM] * 6,
        out_specs=(VMEM, VMEM),
        scratch_shapes=[pltpu.VMEM((2, 4, 16, 16, 128), f32), pltpu.VMEM((2, 16, 4, 16, 128), f32)],
        compiler_params=params(16),
        name="bond_outputs",
    )(pos, ints, pay, *rides, got)


def shift(values, axis, by):
    n = lax.axis_size(axis)
    return lax.ppermute(values, axis, [(i, (i + by) % n) for i in range(n)])


def across(values, axis):
    return lax.all_to_all(values, axis, 0, 0, tiled=True)


def gather(copies, own):
    target = across(copies, ROW)
    near = shift(own, "core", 1)
    pair = jnp.concatenate([own, near], 0)
    return target, (pair, *(shift(pair, "y", k) for k in (1, 2, 3)))


def scatter(pot, keep, send):
    got = across(pot, ROW)
    total = keep + shift(send, "core", 1)
    return got, (total[0], *(shift(total[k], "y", k) for k in (1, 2, 3)))


def on_device(
    charge_drive,
    hardness,
    bond_stiffness,
    coulomb_tiles,
    tile_rows,
    tile_cols,
    tile_count,
    link_bonds,
    link_cells,
    link_ends,
    link_carry,
    link_count,
):
    row = lax.axis_index("x") * 4 + lax.axis_index("z")
    pos = jnp.stack([row, lax.axis_index("y"), lax.axis_index("core")]).astype(jnp.int32)
    links, own_stiffs, order = pack(
        link_count, link_cells, link_bonds, link_ends, link_carry, bond_stiffness, charge_drive
    )
    pay = across(links, ROW)
    drive, hard, own_stiffs, tiles = halves(coulomb_tiles, charge_drive, hardness, own_stiffs)
    ints = jnp.concatenate([tile_rows, tile_cols, link_bonds, link_cells, order, tile_count, link_count])
    meta = pay[:, META, :64].astype(jnp.int32).reshape(16 * 64)
    items, places, number, q_copies, q0 = first(meta, pay, drive, own_stiffs)
    maps = (pos, ints)
    target, pieces = gather(q_copies, q0)
    zeros = jnp.zeros((16, 128), f32)
    *partial, stiffs = tile_products(1, *maps, target, pieces, zeros, drive, tiles)
    stiffs = stiffs.reshape(16, 32, 128)
    pots, parts = scatter(*partial)
    q_copies, q1, v0, sums, ride1 = second(items, places, number, pay, stiffs, drive, q0, hard, pots, parts)
    target, pieces = gather(q_copies, q1)
    *partial, ride2 = tile_products(2, *maps, target, pieces, sums, v0, tiles)
    pots, parts = scatter(*partial)
    copies, ride3 = third(drive, q1, hard, pots, parts)
    got = across(copies, ROW)
    rides = (stiffs, ride1, ride2, ride3)
    keep, send = last(pos, ints, pay, rides, got)
    total = keep + shift(send, "core", 1)
    total = total[0] + shift(total[1], "y", 1) + shift(total[2], "y", 2) + shift(total[3], "y", 3)
    return total[:8], total[8:]


def solution(mesh):
    wide = Mesh(mesh.devices.reshape(4, 4, 4, 2), ALL)
    return jax.shard_map(
        on_device,
        mesh=wide,
        in_specs=(
            P(ALL, None, None),
            P(ALL, None),
            P(ROW, None),
            P(ALL, None, None),
            P(ALL),
            P(ALL),
            P(ALL),
            P(ALL),
            P(ALL),
            P(ALL, None, None),
            P(ALL, None),
            P(ALL),
        ),
        out_specs=(P(ALL, None, None), P(ALL, None, None)),
        check_vma=False,
    )
```

```python
import functools

import jax
import jax.numpy as jnp
from jax import lax
from jax.experimental import pallas as pl
from jax.experimental.pallas import tpu as pltpu
from jax.sharding import Mesh, PartitionSpec as P

f32 = jnp.float32
bf16 = jnp.bfloat16
ROW = ("x", "z")
ALL = ("x", "z", "y", "core")
NN = (((1,), (0,)), ((), ()))
NT = (((1,), (1,)), ((), ()))
SMEM = pl.BlockSpec(memory_space=pltpu.SMEM)
VMEM = pl.BlockSpec(memory_space=pltpu.VMEM)
HBM = pl.BlockSpec(memory_space=pltpu.HBM)
META = 64
PAY = 88
SPACE = 2 * 128


def shape(*dims):
    return jax.ShapeDtypeStruct(dims, f32)


def params(mib):
    return pltpu.CompilerParams(vmem_limit_bytes=mib << 20)


def split(values):
    high = values.astype(bf16)
    return high, (values - high.astype(f32)).astype(bf16)


def stacked(values):
    high, low = split(values)
    return jnp.concatenate([high, low], 0)


def dot(a, b, dims):
    return lax.dot_general(a, b, dims, preferred_element_type=f32)


def ends_matrix(gain, lose):
    atoms = lax.broadcasted_iota(jnp.int32, (128, 128), 0).astype(f32)
    one, zero = f32(1.0), f32(0.0)
    return (jnp.where(atoms == gain, one, zero) - jnp.where(atoms == lose, one, zero)).astype(bf16)


def started(*pairs_and_sems):
    copies = [pltpu.make_async_copy(*each) for each in pairs_and_sems]
    for copy in copies:
        copy.start()
    return copies


def pack_kernel(count_in, cells_in, bonds_in, ends_in, carry_in, stiff_in, drive_in,
                out, stiffs, order, own, count, cells, bonds, ends, carry, stiff, drive, begin, sems):
    copies = started(
        (count_in, count, sems.at[0]),
        (cells_in, cells, sems.at[1]),
        (bonds_in, bonds, sems.at[2]),
        (ends_in, ends, sems.at[3]),
        (carry_in, carry, sems.at[4]),
        (stiff_in, stiff, sems.at[5]),
        (drive_in.at[0], drive, sems.at[6]),
    )
    for copy in copies:
        copy.wait()
    live = count[0]
    owners = [jnp.where(s < live, cells[s] // 4, 16) for s in range(32)]
    for k in range(18):
        begin[k] = 0
    for owner in owners:
        begin[owner + 1] = begin[owner + 1] + 1
    for k in range(1, 18):
        begin[k] = begin[k] + begin[k - 1]
    firsts = [begin[k] for k in range(17)]
    slot = lax.broadcasted_iota(jnp.int32, (32, 128), 0)
    carried = (carry[...] > 0) & (slot < live)
    gain = jnp.where(carried, ends[:, 0, :].astype(f32), -1.0)
    lose = jnp.where(carried, ends[:, 1, :].astype(f32), -1.0)
    lane = lax.broadcasted_iota(jnp.int32, (8, 128), 1)
    named = jnp.zeros((8, 128), jnp.int32)
    for s in range(32):
        to = begin[owners[s]]
        begin[owners[s]] = to + 1
        order[to] = s
        own[pl.ds(to, 1), :] = gain[s : s + 1]
        own[pl.ds(32 + to, 1), :] = lose[s : s + 1]
        stiffs[pl.ds(to, 1), :] = stiff[pl.ds(bonds[s], 1), :]
        named = jnp.where(lane == 32 + to, cells[s] % 4, named)
    for k in range(16):
        out[k, 0:META] = own[...]
        row = jnp.where(lane == 0, firsts[k], jnp.where(lane == 1, firsts[k + 1] - firsts[k], named))
        out[k, META : META + 8] = row.astype(f32)
        out[k, META + 8 : PAY] = drive[...]


def pack(count, cells, bonds, ends, carry, stiff, drive):
    return pl.pallas_call(
        pack_kernel,
        out_shape=(shape(16, PAY, 128), shape(32, 128), jax.ShapeDtypeStruct((32,), jnp.int32)),
        in_specs=[HBM] * 7,
        out_specs=(VMEM, VMEM, SMEM),
        scratch_shapes=[
            pltpu.VMEM((META, 128), f32),
            pltpu.SMEM((1,), jnp.int32),
            pltpu.SMEM((32,), jnp.int32),
            pltpu.SMEM((32,), jnp.int32),
            pltpu.VMEM((32, 2, 128), jnp.int32),
            pltpu.VMEM((32, 128), jnp.int32),
            pltpu.VMEM((64, 128), f32),
            pltpu.VMEM((16, 128), f32),
            pltpu.SMEM((32,), jnp.int32),
            pltpu.SemaphoreType.DMA((7,)),
        ],
        compiler_params=params(56),
        name="pack_links",
    )(count, cells, bonds, ends, carry, stiff, drive)


CHUNK = 16
TILES = 128
CHUNKS = TILES // CHUNK
BONDS, CELLS, ORDER, LIVE_TILES, LIVE_LINKS = 256, 288, 320, 352, 353


def halves_kernel(tiles, drive, hard, stiffs, drive_out, hard_out, stiffs_out, out, whole, halved, in_sems, out_sems):

    def fetch(k):
        part = pl.ds(k * CHUNK, CHUNK)
        return pltpu.make_async_copy(tiles.at[part], whole.at[part], in_sems.at[k])

    def give(k):
        part = pl.ds(k * CHUNK, CHUNK)
        return pltpu.make_async_copy(halved.at[part], out.at[part], out_sems.at[k])

    for k in range(CHUNKS):
        fetch(k).start()
    drive_out[...] = drive[...]
    hard_out[...] = hard[...]
    stiffs_out[...] = stiffs[...]

    def step(k, carry):
        fetch(k).wait()
        for u in range(CHUNK):
            high, low = split(whole[k * CHUNK + u])
            halved[k * CHUNK + u, 0:128] = high
            halved[k * CHUNK + u, 128:256] = low
        give(k).start()
        return carry

    lax.fori_loop(0, CHUNKS, step, 0)
    for k in range(CHUNKS):
        give(k).wait()


def halves(tiles, drive, hard, stiffs):
    return pl.pallas_call(
        halves_kernel,
        out_shape=(
            shape(4, 16, 128),
            shape(4, 128),
            shape(32, 128),
            jax.ShapeDtypeStruct((SPACE, 256, 128), bf16),
        ),
        in_specs=[HBM, VMEM, VMEM, VMEM],
        out_specs=(VMEM, VMEM, VMEM, HBM),
        scratch_shapes=[
            pltpu.VMEM((TILES, 128, 128), f32),
            pltpu.VMEM((TILES, 256, 128), bf16),
            pltpu.SemaphoreType.DMA((CHUNKS,)),
            pltpu.SemaphoreType.DMA((CHUNKS,)),
        ],
        cost_estimate=pl.CostEstimate(flops=3 << 21, bytes_accessed=16 << 20, transcendentals=0),
        compiler_params=params(52),
        name="tile_halves",
    )(tiles, drive, hard, stiffs)


def slot_rows(pay, item):
    k, s = item // 32, item % 32
    return k, s, pay[k, pl.ds(s, 1), :], pay[k, pl.ds(32 + s, 1), :]


GROUP = 16
LAST_GROUP = 8


def first_kernel(meta, pay, drive, stiffs, items, places, number, q_copies, q_own, left, total):

    def from_sender(k, n):
        begin = meta[k * 64]

        def slot(j, n):
            items[n] = k * 32 + begin + j
            places[n] = meta[k * 64 + 32 + begin + j]
            return n + 1

        return lax.fori_loop(0, meta[k * 64 + 1], slot, n)

    n = lax.fori_loop(0, 16, from_sender, 0)
    number[0] = n
    for i in range(4):
        left[i] = stacked(drive[i])
    total[...] = jnp.zeros_like(total)

    def group(g, carry):
        done = []
        for u in range(GROUP):
            t = g * GROUP + u
            valid = t < n
            item = jnp.where(valid, items[t], 0)
            place = jnp.where(valid, places[t], 4)
            _, _, gain, lose = slot_rows(pay, item)
            matrix = ends_matrix(gain, lose)
            u2 = dot(left[jnp.minimum(place, 3)], matrix, NN)
            back = dot(stacked(-(u2[:16] + u2[16:])), matrix, NT)
            done.append((place, back[:16] + back[16:]))
        for place, back in done:
            total[place] = total[place] + back
        return carry

    lax.fori_loop(0, (n + GROUP - 1) // GROUP, group, 0)
    q_own[...] = total[0:4]
    for k in range(16):
        q_copies[k, 0:4] = total[0:4]
        q_copies[k, 4] = stiffs[0:16]
        q_copies[k, 5] = stiffs[16:32]


def first(meta, pay, drive, stiffs):
    return pl.pallas_call(
        first_kernel,
        out_shape=(
            jax.ShapeDtypeStruct((520,), jnp.int32),
            jax.ShapeDtypeStruct((520,), jnp.int32),
            jax.ShapeDtypeStruct((1,), jnp.int32),
            shape(16, 6, 16, 128),
            shape(4, 16, 128),
        ),
        in_specs=[SMEM, VMEM, VMEM, VMEM],
        out_specs=(SMEM, SMEM, SMEM, VMEM, VMEM),
        scratch_shapes=[
            pltpu.VMEM((4, 32, 128), bf16),
            pltpu.VMEM((5, 16, 128), f32),
        ],
        compiler_params=params(16),
        name="first_charges",
    )(meta, pay, drive, stiffs)


def tiles_kernel(begin, pos, ints, target, p0, p1, p2, p3, sums, ride, halved,
                 pot_out, keep, send, rode, tiles, sems, left_s, left_t, pot, mir):
    def fetch(k):
        part = pl.ds(k * CHUNK, CHUNK)
        return pltpu.make_async_copy(halved.at[part], tiles.at[part], sems.at[k])

    for k in range(CHUNKS):
        fetch(k).start()
    rode[...] = target[:, 4:6]
    y, core = pos[1], pos[2]

    def put(ref, at, values):
        high, low = split(values)
        ref[at, 0:16, 0:128] = high
        ref[at, 16:32, 0:128] = low
        ref[at, 0:16, 128:256] = high
        ref[at, 16:32, 128:256] = jnp.zeros_like(low)

    for i in range(64):
        put(left_t, i, target[i // 4, i % 4])
    for k, pair in enumerate((p0, p1, p2, p3)):
        there = (y + 4 - k) % 4
        for i in range(4):
            put(left_s, (there * 2 + core) * 4 + i, pair[i])
            put(left_s, (there * 2 + 1 - core) * 4 + i, pair[4 + i])
    pot[...] = jnp.zeros_like(pot)
    mir[...] = jnp.zeros_like(mir)
    live = ints[LIVE_TILES]

    def group(g, carry):
        fetch(2 * g).wait()
        fetch(2 * g + 1).wait()
        done = []
        for u in range(2 * CHUNK):
            t = g * 2 * CHUNK + u
            row, col = ints[t], ints[TILES + t]
            high, low = tiles[t, 0:128], tiles[t, 128:256]
            p = dot(left_s[col], jnp.concatenate([high.T, low.T], 0), NN)
            m = dot(left_t[row], tiles[t], NN)
            alive = t < live
            done.append((jnp.where(alive, row, 64), jnp.where(alive, col, 32), p[:16] + p[16:], m[:16] + m[16:]))
        for row, col, p, m in done:
            pot[row] = pot[row] + p
            mir[col] = mir[col] + m
        return carry

    def drain(k, carry):
        fetch(k).wait()
        return carry

    groups = (live + 2 * CHUNK - 1) // (2 * CHUNK)
    lax.fori_loop(0, groups, group, 0)
    lax.fori_loop(2 * groups, CHUNKS, drain, 0)
    for k in range(16):
        pot_out[k, 0:4] = pot[4 * k : 4 * k + 4]
        pot_out[k, 4:6] = ride[begin : begin + 2]
    quad = [jnp.zeros((16, 128), f32) for _ in range(4)]
    for i in range(64):
        quad[i % 4] = quad[i % 4] + target[i // 4, i % 4] * pot[i]
    quad = 2.0 * jnp.sum((quad[0] + quad[1]) + (quad[2] + quad[3]), axis=1, keepdims=True)
    lane = lax.broadcasted_iota(jnp.int32, (16, 128), 1)
    all_sums = sums[...] + jnp.where(lane == 3, quad, 0.0)
    for k in range(4):
        there = (y + k) % 4
        for i in range(4):
            keep[k, i] = mir[(there * 2 + core) * 4 + i]
            send[k, i] = mir[(there * 2 + 1 - core) * 4 + i]
        keep[k, 4] = all_sums
        send[k, 4] = all_sums


def tile_products(begin, pos, ints, target, pieces, sums, ride, tiles):
    return pl.pallas_call(
        functools.partial(tiles_kernel, begin),
        out_shape=(shape(16, 6, 16, 128), shape(4, 5, 16, 128), shape(4, 5, 16, 128), shape(16, 2, 16, 128)),
        in_specs=[SMEM] * 2 + [VMEM] * 7 + [HBM],
        out_specs=(VMEM, VMEM, VMEM, VMEM),
        scratch_shapes=[
            pltpu.VMEM((TILES, 256, 128), bf16),
            pltpu.SemaphoreType.DMA((CHUNKS,)),
            pltpu.VMEM((32, 32, 256), bf16),
            pltpu.VMEM((64, 32, 256), bf16),
            pltpu.VMEM((65, 16, 128), f32),
            pltpu.VMEM((33, 16, 128), f32),
        ],
        compiler_params=params(44),
        name="tile_products",
    )(pos, ints, target, *pieces, sums, ride, tiles)


def summed(i, q, hard, pots, s0, s1, s2, s3):
    parts = [pots[k, i] for k in range(16)] + [s0[i], s1[i], s2[i], s3[i], hard[i : i + 1] * q[i]]
    while len(parts) > 1:
        parts = [a + b for a, b in zip(parts[::2], parts[1::2])] + ([parts[-1]] if len(parts) % 2 else [])
    return parts[0]


def second_kernel(items, places, number, pay, stiffs, drive, q, hard, pots, s0, s1, s2, s3,
                  q_copies, q_own, v_own, sums, rode, left, total, acc):
    rode[...] = pots[:, 4:6]
    n = number[0]
    total[...] = jnp.zeros_like(total)
    acc[...] = jnp.zeros_like(acc)
    for i in range(4):
        v = summed(i, q, hard, pots, s0, s1, s2, s3)
        v_own[i] = v
        left[i, 0:32] = stacked(drive[i])
        left[i, 32:64] = stacked(v)

    def group(g, carry):
        done = []
        m = [None] * 4
        for u in range(GROUP):
            t = g * GROUP + u
            valid = t < n
            item = jnp.where(valid, items[t], 0)
            place = jnp.where(valid, places[t], 4)
            k, s, gain, lose = slot_rows(pay, item)
            stiff = stiffs[k, pl.ds(s, 1), :]
            gain = jnp.where(valid, gain, -1.0)
            lose = jnp.where(valid, lose, -1.0)
            matrix = ends_matrix(gain, lose)
            both = dot(left[jnp.minimum(place, 3)], matrix, NN)
            r = -(both[0:16] + both[16:32])
            w = (both[32:48] + both[48:64]) + stiff * r
            back = dot(stacked(w), matrix, NT)
            done.append((place, back[:16] + back[16:]))
            terms = (r * r, r * w, w * w, stiff * (w * w))
            m = [b if a is None else a + b for a, b in zip(m, terms)]
        for place, back in done:
            total[place] = total[place] + back
        for j in range(4):
            acc[j] = acc[j] + m[j]
        return carry

    lax.fori_loop(0, (n + GROUP - 1) // GROUP, group, 0)
    q_own[...] = total[0:4]
    for k in range(16):
        q_copies[k, 0:4] = total[0:4]
        q_copies[k, 4:6] = v_own[0:2]
    lane = lax.broadcasted_iota(jnp.int32, (16, 128), 1)
    diag = acc[3]
    for i in range(4):
        diag = diag + hard[i : i + 1] * (total[i] * total[i])
    out = jnp.zeros((16, 128), f32)
    for j, value in enumerate((acc[0], acc[1], acc[2], diag)):
        out = jnp.where(lane == j, jnp.sum(value, axis=1, keepdims=True), out)
    sums[...] = out


def second(items, places, number, pay, stiffs, drive, q, hard, pots, pieces):
    return pl.pallas_call(
        second_kernel,
        out_shape=(
            shape(16, 6, 16, 128),
            shape(4, 16, 128),
            shape(4, 16, 128),
            shape(16, 128),
            shape(16, 2, 16, 128),
        ),
        in_specs=[SMEM] * 3 + [VMEM] * 10,
        out_specs=(VMEM,) * 5,
        scratch_shapes=[
            pltpu.VMEM((4, 64, 128), bf16),
            pltpu.VMEM((5, 16, 128), f32),
            pltpu.VMEM((4, 16, 128), f32),
        ],
        compiler_params=params(16),
        name="second_charges",
    )(items, places, number, pay, stiffs, drive, q, hard, pots, *pieces)


def third_kernel(drive, q, hard, pots, s0, s1, s2, s3, out, rode):
    rode[...] = pots[:, 4:6]
    sums = (s0[4] + s1[4]) + (s2[4] + s3[4])
    for k in range(16):
        out[k, 4] = sums
        out[k, 5] = drive[3]
    for i in range(4):
        v = summed(i, q, hard, pots, s0, s1, s2, s3)
        for k in range(16):
            out[k, i] = v


def third(drive, q, hard, pots, pieces):
    return pl.pallas_call(
        third_kernel,
        out_shape=(shape(16, 6, 16, 128), shape(16, 2, 16, 128)),
        in_specs=[VMEM] * 8,
        out_specs=(VMEM, VMEM),
        compiler_params=params(16),
        name="potentials_out",
    )(drive, q, hard, pots, *pieces)


def last_kernel(pos, ints, pay, stiffs, a1, b0, b1, got, keep, send, out, held):
    n = ints[LIVE_LINKS]
    row, core = pos[0], pos[2]
    sums = got[0, 4]
    for k in range(1, 16):
        sums = sums + got[k, 4]
    m0, m1, m2, m3 = (sums[:, j : j + 1] for j in range(4))
    step0 = m0 / m1
    norm1 = m0 - 2.0 * step0 * m1 + step0 * step0 * m2
    ratio = norm1 / m0
    grow = 1.0 + ratio
    step1 = norm1 / (grow * grow * m1 - 2.0 * step0 * grow * m2 + step0 * step0 * m3)
    wide = lambda a: jnp.broadcast_to(a, (16, 128))
    sol_r, sol_w = wide(step0 + step1 * grow), wide(-step1 * step0)
    res_w, res_z = wide(-step0 - step1 * grow), wide(step1 * step0)
    out[...] = jnp.zeros_like(out)
    for k in range(16):
        held[0, k, 0] = pay[k, META + 8 : PAY]
        held[0, k, 3] = got[k, 5]
    held[0, :, 1:3] = a1[...]
    held[1, :, 0:2] = b0[...]
    held[1, :, 2:4] = b1[...]

    def group(g, carry):
        done = []
        for u in range(LAST_GROUP):
            t = g * LAST_GROUP + u
            valid = t < n
            s = jnp.where(valid, t, 0)
            named = ints[ORDER + s]
            cell, block = ints[CELLS + named], ints[BONDS + named]
            k, i = cell // 4, cell % 4
            gain, lose = pay[row, pl.ds(s, 1), :], pay[row, pl.ds(32 + s, 1), :]
            stiff = stiffs[row, pl.ds(s, 1), :]
            gain = jnp.where(valid, gain, -1.0)
            lose = jnp.where(valid, lose, -1.0)
            matrix = ends_matrix(gain, lose)
            left = jnp.concatenate([stacked(held[0, k, i]), stacked(held[1, k, i]), stacked(got[k, i])], 0)
            b = dot(left, matrix, NN)
            r = -(b[0:16] + b[16:32])
            w = (b[32:48] + b[48:64]) + stiff * r
            z = (b[64:80] + b[80:96]) + stiff * w
            away = jnp.where((block // 8) % 2 == core, 0, 1)
            done.append((away, (block // 16 + 4 - pos[1]) % 4, block % 8, sol_r * r + sol_w * w, r + res_w * w + res_z * z))
        for away, there, at, sol, res in done:
            out[away, there, at] = out[away, there, at] + sol
            out[away, there, 8 + at] = out[away, there, 8 + at] + res
        return carry

    lax.fori_loop(0, (n + LAST_GROUP - 1) // LAST_GROUP, group, 0)
    keep[...] = out[0]
    send[...] = out[1]


def last(pos, ints, pay, rides, got):
    return pl.pallas_call(
        last_kernel,
        out_shape=(shape(4, 16, 16, 128), shape(4, 16, 16, 128)),
        in_specs=[SMEM] * 2 + [VMEM] * 6,
        out_specs=(VMEM, VMEM),
        scratch_shapes=[pltpu.VMEM((2, 4, 16, 16, 128), f32), pltpu.VMEM((2, 16, 4, 16, 128), f32)],
        compiler_params=params(16),
        name="bond_outputs",
    )(pos, ints, pay, *rides, got)


def shift(values, axis, by):
    n = lax.axis_size(axis)
    return lax.ppermute(values, axis, [(i, (i + by) % n) for i in range(n)])


def across(values, axis):
    return lax.all_to_all(values, axis, 0, 0, tiled=True)


def gather(copies, own):
    target = across(copies, ROW)
    near = shift(own, "core", 1)
    pair = jnp.concatenate([own, near], 0)
    return target, (pair, *(shift(pair, "y", k) for k in (1, 2, 3)))


def scatter(pot, keep, send):
    got = across(pot, ROW)
    total = keep + shift(send, "core", 1)
    return got, (total[0], *(shift(total[k], "y", k) for k in (1, 2, 3)))


def on_device(
    charge_drive,
    hardness,
    bond_stiffness,
    coulomb_tiles,
    tile_rows,
    tile_cols,
    tile_count,
    link_bonds,
    link_cells,
    link_ends,
    link_carry,
    link_count,
):
    row = lax.axis_index("x") * 4 + lax.axis_index("z")
    pos = jnp.stack([row, lax.axis_index("y"), lax.axis_index("core")]).astype(jnp.int32)
    links, own_stiffs, order = pack(
        link_count, link_cells, link_bonds, link_ends, link_carry, bond_stiffness, charge_drive
    )
    pay = across(links, ROW)
    drive, hard, own_stiffs, tiles = halves(coulomb_tiles, charge_drive, hardness, own_stiffs)
    ints = jnp.concatenate([tile_rows, tile_cols, link_bonds, link_cells, order, tile_count, link_count])
    meta = pay[:, META, :64].astype(jnp.int32).reshape(16 * 64)
    items, places, number, q_copies, q0 = first(meta, pay, drive, own_stiffs)
    maps = (pos, ints)
    target, pieces = gather(q_copies, q0)
    zeros = jnp.zeros((16, 128), f32)
    *partial, stiffs = tile_products(1, *maps, target, pieces, zeros, drive, tiles)
    stiffs = stiffs.reshape(16, 32, 128)
    pots, parts = scatter(*partial)
    q_copies, q1, v0, sums, ride1 = second(items, places, number, pay, stiffs, drive, q0, hard, pots, parts)
    target, pieces = gather(q_copies, q1)
    *partial, ride2 = tile_products(2, *maps, target, pieces, sums, v0, tiles)
    pots, parts = scatter(*partial)
    copies, ride3 = third(drive, q1, hard, pots, parts)
    got = across(copies, ROW)
    rides = (stiffs, ride1, ride2, ride3)
    keep, send = last(pos, ints, pay, rides, got)
    total = keep + shift(send, "core", 1)
    total = total[0] + shift(total[1], "y", 1) + shift(total[2], "y", 2) + shift(total[3], "y", 3)
    return total[:8], total[8:]


def solution(mesh):
    wide = Mesh(mesh.devices.reshape(4, 4, 4, 2), ALL)
    return jax.shard_map(
        on_device,
        mesh=wide,
        in_specs=(
            P(ALL, None, None),
            P(ALL, None),
            P(ROW, None),
            P(ALL, None, None),
            P(ALL),
            P(ALL),
            P(ALL),
            P(ALL),
            P(ALL),
            P(ALL, None, None),
            P(ALL, None),
            P(ALL),
        ),
        out_specs=(P(ALL, None, None), P(ALL, None, None)),
        check_vma=False,
    )
```
